32 devices in a mesh: dp: 8 (over z, x), tensor: 4 (over y, core).
Axes of the slice: x: 2, y: 2, z: 4, core: 2. Of those that a mesh axis runs over, the one named last changes fastest.
Arguments:
- tokens: bfloat16 [16384, 768], P('dp'), may hold values from -6 to 6
- attn_gain: float32 [768], replicated, may hold values from 0.5 to 1.5
- qkv_weight: bfloat16 [3, 768, 768], P(None, None, 'tensor'), may hold values from -0.21875 to 0.21875
- proj_weight: bfloat16 [768, 768], P(None, 'tensor'), may hold values from -3.5 to 3.5
- bias_table: float32 [12, 32], P('tensor'), may hold values from -4 to 4
- buckets: int32 [2047], replicated, may hold values from 0 to 31
- ffn_gain: float32 [768], replicated, may hold values from 0.5 to 1.5
- router_weight: bfloat16 [768, 4], replicated, may hold values from -0.15625 to 0.15625
- routes: int32 [16384, 1], P('dp'), may hold values from 0 to 3; in each aligned block of 2048 rows (0 to 2047, 2048 to 4095, ...) at most 1024 rows name the same one
- up_weight: bfloat16 [4, 768, 3072], P(None, None, 'tensor'), may hold values from -0.21875 to 0.21875
- down_weight: bfloat16 [4, 768, 3072], P(None, None, 'tensor'), may hold values from -0.4375 to 0.4375
- cotangent: bfloat16 [16384, 768], P(('dp', 'tensor')), may hold values from -6 to 6
Outputs:
- layer_out: bfloat16 [16384, 768], P(('dp', 'tensor'))
- tokens_grad: float32 [16384, 768], P(('dp', 'tensor'))
- attn_gain_grad: float32 [768], replicated
- qkv_grad: float32 [3, 768, 768], P(None, 'dp', 'tensor')
- proj_grad: float32 [768, 768], P('dp', 'tensor')
- table_grad: float32 [12, 32], replicated
- ffn_gain_grad: float32 [768], replicated
- router_grad: float32 [768, 4], replicated
- up_grad: float32 [4, 768, 3072], P(None, 'dp', 'tensor')
- down_grad: float32 [4, 768, 3072], P(None, 'dp', 'tensor')
The draws below stay inside these ranges and needn't reach their ends.
Inputs may be any that keep to these rules, and one draw needn't show every extreme that they name: `routes`: in each aligned block of 2048 rows (the rows of one index of dp) no expert is named by more than 1024 rows; in every draw some block has an expert named by exactly 1024 rows.
All inputs are finite; a program needn't handle non-finite values.
Results may differ from the reference program's by a relative error of at most 0.015.
The reference program's roundings to bfloat16 on the way count: a program that leaves them out, or rounds other values in their place, can miss the bound.
Values may be sent and summed in bfloat16 or wider, within the bound.
No kernel may reach another device: no remote copies, remote signals or barrier semaphores. Data moves between devices by JAX's collectives and lax.ppermute only.
A program may use at most 192 MiB of HBM per device.

```python
import math
import jax
import jax.numpy as jnp
import numpy as np
from jax import lax

D = 768
HEADS = 12
HDIM = 64
FF = 3072
NB = 32
E = 4
SEQ = 1024
SEQS_DEV = 2
ROWS_DEV = 2048
CAP = 1024
TOKENS = 16384
N_DP = 8


def set_ends(entries, own_key, least, largest):
    longest = entries.shape.index(max(entries.shape))
    spots = []
    for shift in (0, 1):
        where = [jax.random.randint(jax.random.fold_in(own_key, axis), (), 0, length) for axis, length in enumerate(entries.shape)]
        where[longest] = (where[longest] + shift) % entries.shape[longest]
        spots.append(tuple(where))
    return entries.at[spots[0]].set(least).at[spots[1]].set(largest)


def level_of(key, dims, pieces, least, top_value):
    loudness, own = 1.0, jax.random.fold_in(key, 6)
    for position, blocks in pieces:
        heights = jnp.exp(jax.random.uniform(jax.random.fold_in(own, position), (blocks,), jnp.float32, least / len(pieces), top_value / len(pieces)))
        loudness = loudness * jnp.repeat(heights, dims[position] // blocks).reshape([-1 if axis == position else 1 for axis in range(len(dims))])
    return loudness


def routed_block(stream_key, own, number, rows, count, top, most, lean):
    ranking = jax.random.permutation(stream_key, count)
    packed, common = load_shares(count, rows * top, most, lean, True), load_shares(count, rows * top, most, lean, False)
    places = jnp.arange(count)

    def named(sizes, rotation):
        used = int((sizes > 0).sum())
        fixed = max(1, used // 4)
        moved = fixed + (places - fixed + rotation * (used - fixed)) % max(1, count - fixed)
        return jnp.zeros((count,), jnp.int32).at[ranking[jnp.where(places < fixed, places, moved)]].set(jnp.asarray(sizes, jnp.int32))

    sizes = jnp.where(number % 4 == 0, named(packed, number // 4), named(common, number - number // 4 - 1))
    mixed = jax.random.permutation(jax.random.fold_in(own, 3), count)
    source_of, receiver = mixed[0:count // 2 * 2:2], mixed[1:count // 2 * 2:2]
    slack = jnp.minimum(sizes[source_of] - 1, most - sizes[receiver]) // 2
    slack = jnp.where((source_of == ranking[0]) | (receiver == ranking[0]) | (sizes[receiver] == 0), 0, jnp.maximum(slack, 0))
    moved = jax.random.randint(jax.random.fold_in(own, 4), (count // 2,), 0, 1 << 20) % (slack + 1)
    sizes = sizes.at[source_of].add(-moved).at[receiver].add(moved)
    items = jnp.searchsorted(jnp.cumsum(sizes), jnp.arange(rows * top), side="right").astype(jnp.int32)
    grid = items.reshape(top, rows).T
    grid = grid[jax.random.permutation(jax.random.fold_in(own, 1), rows)]
    rotation = jax.random.randint(jax.random.fold_in(own, 2), (rows, 1), 0, top)
    return jnp.take_along_axis(grid, (jnp.arange(top)[None, :] + rotation) % top, axis=1)


def load_shares(number_of, total, bound, lean, full):
    weights = [(1 << 20) // math.isqrt(grade ** lean) + 1 for grade in range(1, number_of + 1)]
    largest = bound if full else min(bound, max(-(-total // number_of), total * weights[0] // sum(weights)))
    least = 1 if total - largest >= number_of - 1 else 0
    holding, rest = [largest] + [least] * (number_of - 1), total - largest - least * (number_of - 1)
    while rest > 0:
        free = [i for i in range(1, number_of) if holding[i] < largest] or [i for i in range(1, number_of) if holding[i] < bound]
        pool, budget = sum([weights[i] for i in free]), rest
        for i in free:
            extra = min(bound - holding[i], max(1, budget * weights[i] // pool), rest)
            holding[i] = holding[i] + extra
            rest = rest - extra
    return np.array(holding)


def normal_values(stream_key, extent, width, reach, split=(), dtype=jnp.bfloat16):
    values = jax.random.normal(stream_key, extent, jnp.float32) * width
    if len(split) > 0:
        values = level_of(stream_key, extent, split, -0.22, 0.18) * values
    return jnp.clip(values, min=-reach, max=reach).astype(dtype)


def setup_inputs(seed: int = 0) -> dict:
    arg_keys = jax.random.split(jax.random.key(seed), 13)
    tokens = normal_values(arg_keys[0], (TOKENS, D), 1.0, 6.0, ((0, 8),))
    attn_gain = jnp.clip(1.0 + 0.1 * jax.random.normal(arg_keys[1], (D,), jnp.float32), 0.5, 1.5)
    qkv_weight = normal_values(arg_keys[2], (3, D, HEADS * HDIM), D ** -0.5, 0.21875, ((2, 4),))
    proj_weight = normal_values(arg_keys[3], (D, HEADS * HDIM), (max(D // 256, 1)) ** -0.5, 3.5, ((1, 4),))
    bias_table = normal_values(arg_keys[4], (HEADS, NB), 1.0, 4.0, ((0, 4),), jnp.float32)
    buckets = set_ends(jax.random.randint(arg_keys[5], (2 * SEQ - 1,), 0, NB), jax.random.fold_in(arg_keys[5], 1), 0, NB - 1).astype(jnp.int32)
    ffn_gain = jnp.clip(1.0 + 0.1 * jax.random.normal(arg_keys[6], (D,), jnp.float32), 0.5, 1.5)
    router_weight = normal_values(arg_keys[7], (D, E), (2 * D) ** -0.5, 0.15625)
    routes_keys = jax.random.split(jax.random.fold_in(arg_keys[8], 1), TOKENS // ROWS_DEV)
    routes_turns = jax.random.permutation(jax.random.fold_in(arg_keys[8], 3), TOKENS // ROWS_DEV)
    routes = jax.vmap(lambda own, number: routed_block(jax.random.fold_in(arg_keys[8], 2), own, number, ROWS_DEV, E, 1, CAP, 1))(routes_keys, routes_turns).reshape((TOKENS, 1))
    up_weight = normal_values(arg_keys[9], (E, D, FF), D ** -0.5, 0.21875, ((2, 4),))
    down_weight = normal_values(arg_keys[10], (E, D, FF), (FF // 16) ** -0.5, 0.4375, ((2, 4),))
    cotangent = normal_values(arg_keys[11], (TOKENS, D), 1.0, 6.0, ((0, 32),))
    return dict(tokens=tokens, attn_gain=attn_gain, qkv_weight=qkv_weight, proj_weight=proj_weight, bias_table=bias_table, buckets=buckets, ffn_gain=ffn_gain, router_weight=router_weight, routes=routes, up_weight=up_weight, down_weight=down_weight, cotangent=cotangent)


EPS = 1e-06

@jax.custom_vjp
def low(v):
    return lax.optimization_barrier(v.astype(jnp.bfloat16)).astype(jnp.float32)

@jax.custom_vjp
def low_back(v):
    return v

def low_keep(v):
    return (low(v), None)

def low_pass(kept, grad):
    return (grad,)

def back_keep(v):
    return (v, None)

def back_low(kept, grad):
    return (low(grad),)
low.defvjp(low_keep, low_pass)
low_back.defvjp(back_keep, back_low)

def norm_rows(values, gain_vector):
    return values * lax.rsqrt(lax.optimization_barrier(jnp.mean(values * values, axis=-1, keepdims=True)) + EPS) * gain_vector

def forward(params, inputs, routes_group, buckets):
    attn_gain, qkv_weight, proj_weight, bias_table, ffn_gain, router_weight, up_weight, down_weight = params
    highest = lax.Precision.HIGHEST
    normed_one = low(norm_rows(inputs, attn_gain))
    grid_shape = (SEQS_DEV, SEQ, HEADS, HDIM)
    projected = [low(low_back(jnp.dot(normed_one, qkv_weight[which], precision=highest))).reshape(grid_shape) for which in range(3)]
    queries, key_rows, value_rows = projected
    offsets = jnp.arange(SEQ)[None, :] - jnp.arange(SEQ)[:, None] + SEQ - 1
    position_bias = bias_table[:, buckets[offsets]]
    scores = low_back(HDIM ** (-0.5) * jnp.einsum('sqhd,skhd->shqk', queries, key_rows, precision=highest) + position_bias[None])
    weights = low(jax.nn.softmax(scores, axis=-1))
    attended = low(low_back(jnp.einsum('shqk,skhd->sqhd', weights, value_rows, precision=highest)))
    attended = attended.reshape(ROWS_DEV, HEADS * HDIM)
    attn_out = low_back(jnp.dot(attended, proj_weight.T, precision=highest))
    hidden = inputs + attn_out
    normed_two = low(norm_rows(hidden, ffn_gain))
    logits = low_back(jnp.dot(normed_two, router_weight, precision=highest))
    router_probs = jax.nn.softmax(logits, axis=-1)
    route_hot = (routes_group[:, None] == jnp.arange(E)[None, :]).astype(jnp.float32)
    gate_prob = lax.optimization_barrier(jnp.sum(router_probs * route_hot, axis=-1))
    expert_out = jnp.zeros_like(hidden)
    for expert in range(E):
        pre_act = low_back(jnp.dot(normed_two, up_weight[expert], precision=highest))
        activated = low(jax.nn.gelu(pre_act))
        expert_out = expert_out + route_hot[:, expert:expert + 1] * jnp.dot(activated, down_weight[expert].T, precision=highest)
    expert_out = low_back(expert_out)
    return hidden + gate_prob[:, None] * expert_out

def reference(tokens, attn_gain, qkv_weight, proj_weight, bias_table, buckets, ffn_gain, router_weight, routes, up_weight, down_weight, cotangent):
    params = tuple((weight.astype(jnp.float32) for weight in (attn_gain, qkv_weight, proj_weight, bias_table, ffn_gain, router_weight, up_weight, down_weight)))
    token_groups = tokens.astype(jnp.float32).reshape(N_DP, ROWS_DEV, D)
    route_groups = routes.reshape(N_DP, ROWS_DEV)
    grad_groups = cotangent.astype(jnp.float32).reshape(N_DP, ROWS_DEV, D)

    def group_step(totals, group):
        inputs, routes_group, grad_rows = group
        result, backward = jax.vjp(lambda weights_in, rows_in: forward(weights_in, rows_in, routes_group, buckets), params, inputs)
        weight_grads, input_grad = backward(grad_rows)
        totals = jax.tree.map(jnp.add, totals, weight_grads)
        return (totals, (result.astype(jnp.bfloat16), input_grad))
    zero_grads = jax.tree.map(jnp.zeros_like, params)
    totals, (outputs, input_grads) = lax.scan(group_step, zero_grads, (token_groups, route_groups, grad_groups))
    return (outputs.reshape(TOKENS, D), input_grads.reshape(TOKENS, D), totals[0], totals[1], totals[2], totals[3], totals[4], totals[5], totals[6], totals[7])
```

```python
import functools
import jax, jax.numpy as jnp
from jax import lax
from jax.experimental import pallas as pl
from jax.experimental.pallas import tpu as pltpu
from jax.sharding import PartitionSpec as P

QB = 256
KB = 128


def mm(a, b, dims):
    return lax.dot_general(a, b, (dims, ((), ())), preferred_element_type=jnp.float32)


def score_block(keys, queries, skew, first_query, seq_len):
    scores = mm(keys, queries, ((1,), (0,)))
    bias = [
        skew[:, pl.ds(pl.multiple_of(first_query - first_key + seq_len - KB, KB), QB)]
        for first_key in range(0, seq_len, KB)
    ]
    return scores + jnp.concatenate(bias, axis=0)


def forward_kernel(seq_ref, qkv_ref, offset_ref, mixed_ref, lse_ref, skew):
    seq_len = qkv_ref.shape[2]
    scale = qkv_ref.shape[1] ** -0.5
    skew[...] = pltpu.roll(
        jnp.broadcast_to(offset_ref[0], (KB, 2 * seq_len)), 0, 1, stride=1, stride_axis=0
    )
    keys = qkv_ref[1].T
    values = qkv_ref[2]

    def block(index, carry):
        first = pl.multiple_of(index * QB, QB)
        queries = qkv_ref[0, :, pl.ds(first, QB)] * jnp.bfloat16(scale)
        scores = score_block(keys, queries, skew, first, seq_len)
        largest = jnp.max(scores, axis=0, keepdims=True)
        expos = jnp.exp(scores - largest)
        total = jnp.sum(expos, axis=0, keepdims=True)
        weights = (expos * (1.0 / total)).astype(jnp.bfloat16)
        mixed_ref[:, pl.ds(first, QB)] = mm(values, weights, ((1,), (0,))).astype(jnp.bfloat16)
        lse_ref[0, :, pl.ds(first, QB)] = largest + jnp.log(total)
        return carry

    lax.fori_loop(0, seq_len // QB, block, 0, unroll=True)


def forward_attention(seq, qkv, offsets, seq_len):
    _, width, rows = qkv.shape
    heads = offsets.shape[0]
    size = width // heads
    return pl.pallas_call(
        forward_kernel,
        grid_spec=pltpu.PrefetchScalarGridSpec(
            num_scalar_prefetch=1,
            grid=(heads,),
            in_specs=[
                pl.BlockSpec((3, size, seq_len), lambda h, s: (0, h, s[0])),
                pl.BlockSpec((1, 1, 2 * seq_len), lambda h, s: (h, 0, 0)),
            ],
            out_specs=[
                pl.BlockSpec((size, seq_len), lambda h, s: (h, 0)),
                pl.BlockSpec((1, 1, seq_len), lambda h, s: (h, 0, 0)),
            ],
            scratch_shapes=[pltpu.VMEM((KB, 2 * seq_len), jnp.float32)],
        ),
        out_shape=[
            jax.ShapeDtypeStruct((width, seq_len), jnp.bfloat16),
            jax.ShapeDtypeStruct((heads, 1, seq_len), jnp.float32),
        ],
        compiler_params=pltpu.CompilerParams(vmem_limit_bytes=48 * 2**20),
        name="attention_forward",
    )(seq, qkv, offsets)


def backward_kernel(
    seq_ref, qkv_ref, grad_ref, lse_ref, offset_ref, out_ref, diag_ref, skew, sums, probs_all, score_all
):
    seq_len = qkv_ref.shape[2]
    scale = qkv_ref.shape[1] ** -0.5
    skew[...] = pltpu.roll(
        jnp.broadcast_to(offset_ref[0], (KB, 2 * seq_len)), 0, 1, stride=1, stride_axis=0
    )
    sums[...] = jnp.zeros_like(sums)
    keys_t = qkv_ref[1]
    keys = keys_t.T
    values = qkv_ref[2].T

    def block(index, carry):
        first = pl.multiple_of(index * QB, QB)
        here = pl.ds(first, QB)
        queries = qkv_ref[0, :, here] * jnp.bfloat16(scale)
        scores = score_block(keys, queries, skew, first, seq_len)
        probs = jnp.exp(scores - lse_ref[0, :, here])
        probs_all[:, here] = probs.astype(jnp.bfloat16)
        prob_grad = mm(values, grad_ref[:, here], ((1,), (0,)))
        centre = jnp.sum(probs * prob_grad, axis=0, keepdims=True)
        score_grad = probs * (prob_grad - centre)
        rounded = score_grad.astype(jnp.bfloat16)
        score_all[:, here] = rounded
        for first_key in range(0, seq_len, KB):
            spot = pl.ds(pl.multiple_of(first - first_key + seq_len - KB, KB), QB)
            sums[:, spot] += score_grad[first_key : first_key + KB]
        out_ref[0, :, here] = (mm(keys_t, rounded, ((1,), (0,))) * scale).astype(jnp.bfloat16)
        return carry

    lax.fori_loop(0, seq_len // QB, block, 0, unroll=True)
    queries = qkv_ref[0] * jnp.bfloat16(scale)
    out_ref[1] = mm(queries, score_all[...], ((1,), (1,))).astype(jnp.bfloat16)
    out_ref[2] = mm(grad_ref[...], probs_all[...], ((1,), (1,))).astype(jnp.bfloat16)
    part = sums[...]
    half = KB // 2
    while half >= 1:
        part = part[:half] + pltpu.roll(part[half:], 2 * seq_len - half, 1)
        half //= 2
    diag_ref[0] = part


def backward_attention(seq, qkv, grads, lse, offsets, seq_len):
    _, width, rows = qkv.shape
    heads = offsets.shape[0]
    size = width // heads
    return pl.pallas_call(
        backward_kernel,
        grid_spec=pltpu.PrefetchScalarGridSpec(
            num_scalar_prefetch=1,
            grid=(heads,),
            in_specs=[
                pl.BlockSpec((3, size, seq_len), lambda h, s: (0, h, s[0])),
                pl.BlockSpec((size, seq_len), lambda h, s: (h, 0)),
                pl.BlockSpec((1, 1, seq_len), lambda h, s: (h, 0, 0)),
                pl.BlockSpec((1, 1, 2 * seq_len), lambda h, s: (h, 0, 0)),
            ],
            out_specs=[
                pl.BlockSpec((3, size, seq_len), lambda h, s: (0, h, 0)),
                pl.BlockSpec((1, 1, 2 * seq_len), lambda h, s: (h, 0, 0)),
            ],
            scratch_shapes=[
                pltpu.VMEM((KB, 2 * seq_len), jnp.float32),
                pltpu.VMEM((KB, 2 * seq_len), jnp.float32),
                pltpu.VMEM((seq_len, seq_len), jnp.bfloat16),
                pltpu.VMEM((seq_len, seq_len), jnp.bfloat16),
            ],
        ),
        out_shape=[
            jax.ShapeDtypeStruct((3, width, seq_len), jnp.bfloat16),
            jax.ShapeDtypeStruct((heads, 1, 2 * seq_len), jnp.float32),
        ],
        compiler_params=pltpu.CompilerParams(vmem_limit_bytes=48 * 2**20),
        name="attention_backward",
    )(seq, qkv, grads, lse, offsets)


CH = 16
TM = 128


def tile_limit(rows, shares, experts):
    chunks = rows // CH + shares * (experts - 1)
    return (chunks + experts * (TM // CH - 1)) // (TM // CH)


def plan_segments(counts):
    starts = jnp.cumsum(counts, axis=1) - counts
    first = starts // CH
    chunks = jnp.where(counts > 0, (starts + counts + CH - 1) // CH - first, 0)
    tiles = (jnp.sum(chunks, axis=0) * CH + TM - 1) // TM
    base = jnp.cumsum(tiles) - tiles
    return jnp.concatenate(
        [first, chunks, starts, starts + counts, tiles[None], base[None]], axis=0
    ).astype(jnp.int32)


def expert_kernel(
    plan_ref, x_ref, c_ref, router_ref, up_ref, down_ref,
    y_ref, back_ref, gate_ref, xs_ref, ms_ref, dys_ref, dus_ref,
    cs, ybuf, bbuf, gbuf, *, shares,
):
    expert = pl.program_id(0)
    share_rows = x_ref.shape[0] // shares
    tiles = plan_ref[4 * shares, expert]
    base = plan_ref[4 * shares + 1, expert] * TM

    @pl.when(expert == 0)
    def _():
        y_ref[...] = jnp.zeros_like(y_ref)
        back_ref[...] = jnp.zeros_like(back_ref)
        gate_ref[...] = jnp.zeros_like(gate_ref)

    filled = 0
    for share in range(shares):
        first = plan_ref[share, expert]
        chunks = plan_ref[shares + share, expert]
        start = plan_ref[2 * shares + share, expert]
        end = plan_ref[3 * shares + share, expert]

        def gather(index, carry, share=share, first=first, start=start, end=end, filled=filled):
            here = (first + index) * CH
            source = pl.ds(pl.multiple_of(here + share * share_rows, CH), CH)
            local = pl.multiple_of((filled + index) * CH, CH)
            row = here + lax.broadcasted_iota(jnp.int32, (CH, 1), 0)
            keep = (row >= start) & (row < end)
            zero = jnp.zeros((), jnp.bfloat16)
            xs_ref[pl.ds(pl.multiple_of(base + local, CH), CH)] = jnp.where(keep, x_ref[source], zero)
            cs[pl.ds(local, CH)] = jnp.where(keep, c_ref[source], zero)
            return carry

        lax.fori_loop(0, chunks, gather, 0)
        filled = filled + chunks

    def clear(index, carry):
        local = pl.multiple_of(index * CH, CH)
        xs_ref[pl.ds(pl.multiple_of(base + local, CH), CH)] = jnp.zeros((CH, xs_ref.shape[1]), jnp.bfloat16)
        cs[pl.ds(local, CH)] = jnp.zeros((CH, cs.shape[1]), jnp.bfloat16)
        return carry

    lax.fori_loop(filled, tiles * (TM // CH), clear, 0)

    def tile(index, carry):
        local = pl.ds(pl.multiple_of(index * TM, TM), TM)
        saved = pl.ds(pl.multiple_of(base + index * TM, TM), TM)
        x = xs_ref[saved]
        c = cs[local]
        logits = mm(x, router_ref[...], ((1,), (0,)))
        lane = lax.broadcasted_iota(jnp.int32, logits.shape, 1)
        logits = jnp.where(lane < EXPERTS, logits, -jnp.inf)
        expos = jnp.exp(logits - jnp.max(logits, axis=1, keepdims=True))
        mine = jnp.sum(jnp.where(lane == expert, expos, 0.0), axis=1, keepdims=True)
        gate = mine / jnp.sum(expos, axis=1, keepdims=True)
        c32 = c.astype(jnp.float32)
        dy = (gate * c32).astype(jnp.bfloat16)
        dys_ref[saved] = dy
        u = mm(x, up_ref[0], ((1,), (0,)))
        root = 0.7978845608028654
        square = u * u
        bent = jnp.tanh(root * (u * (1.0 + 0.044715 * square)))
        half = 0.5 * (1.0 + bent)
        m = (u * half).astype(jnp.bfloat16)
        ms_ref[saved] = m
        slope = half + (0.5 * root) * (u * ((1.0 - bent * bent) * (1.0 + (3 * 0.044715) * square)))
        y = mm(m, down_ref[0], ((1,), (1,)))
        ybuf[local] = y
        gbuf[local] = jnp.broadcast_to(jnp.sum(y * c32, axis=1, keepdims=True), (TM, gbuf.shape[1]))
        dm = mm(dy, down_ref[0], ((1,), (0,)))
        du = (slope * dm).astype(jnp.bfloat16)
        dus_ref[saved] = du
        bbuf[local] = mm(du, up_ref[0], ((1,), (1,)))
        return carry

    lax.fori_loop(0, tiles, tile, 0)

    filled = 0
    for share in range(shares):
        first = plan_ref[share, expert]
        chunks = plan_ref[shares + share, expert]

        def scatter(index, carry, share=share, first=first, filled=filled):
            target = pl.ds(pl.multiple_of((first + index) * CH + share * share_rows, CH), CH)
            local = pl.ds(pl.multiple_of((filled + index) * CH, CH), CH)
            y_ref[target] += ybuf[local]
            back_ref[target] += bbuf[local]
            gate_ref[target] += gbuf[local]
            return carry

        lax.fori_loop(0, chunks, scatter, 0)
        filled = filled + chunks

EXPERTS = 4

def run_experts(plan, x, c, router, up, down, shares):
    rows, width = x.shape
    experts, _, hidden = up.shape
    saved = tile_limit(rows, shares, experts) * TM
    most = -(-rows // TM) * TM
    whole = lambda shape: pl.BlockSpec(shape, lambda e, p: (0, 0))
    brain = jnp.bfloat16
    return pl.pallas_call(
        functools.partial(expert_kernel, shares=shares),
        grid_spec=pltpu.PrefetchScalarGridSpec(
            num_scalar_prefetch=1,
            grid=(experts,),
            in_specs=[
                whole((rows, width)),
                whole((rows, width)),
                whole(router.shape),
                pl.BlockSpec((1, width, hidden), lambda e, p: (e, 0, 0)),
                pl.BlockSpec((1, width, hidden), lambda e, p: (e, 0, 0)),
            ],
            out_specs=[
                whole((rows, width)), whole((rows, width)), whole((rows, 128)),
                whole((saved, width)), whole((saved, hidden)), whole((saved, width)), whole((saved, hidden)),
            ],
            scratch_shapes=[
                pltpu.VMEM((most, width), brain),
                pltpu.VMEM((most, width), jnp.float32),
                pltpu.VMEM((most, width), jnp.float32),
                pltpu.VMEM((most, 128), jnp.float32),
            ],
        ),
        out_shape=[
            jax.ShapeDtypeStruct((rows, width), jnp.float32),
            jax.ShapeDtypeStruct((rows, width), jnp.float32),
            jax.ShapeDtypeStruct((rows, 128), jnp.float32),
            jax.ShapeDtypeStruct((saved, width), brain),
            jax.ShapeDtypeStruct((saved, hidden), brain),
            jax.ShapeDtypeStruct((saved, width), brain),
            jax.ShapeDtypeStruct((saved, hidden), brain),
        ],
        compiler_params=pltpu.CompilerParams(vmem_limit_bytes=56 * 2**20),
        cost_estimate=pl.CostEstimate(flops=8 * rows * width * hidden, bytes_accessed=30 * 2**20, transcendentals=0),
        name="experts",
    )(plan, x, c, router, up, down)


def grads_kernel(*refs, halves, plan_row):
    plans = refs[:halves]
    data = refs[halves : halves + 4 * halves]
    up_out, down_out, up_acc, down_acc = refs[5 * halves :]
    expert = pl.program_id(0)
    up_acc[...] = jnp.zeros_like(up_acc)
    down_acc[...] = jnp.zeros_like(down_acc)
    for half in range(halves):
        x_ref, m_ref, dy_ref, du_ref = data[4 * half : 4 * half + 4]
        tiles = plans[half][plan_row, expert]
        base = plans[half][plan_row + 1, expert] * TM

        def tile(index, carry, x_ref=x_ref, m_ref=m_ref, dy_ref=dy_ref, du_ref=du_ref, base=base):
            here = pl.ds(pl.multiple_of(base + index * TM, TM), TM)
            up_acc[...] += mm(x_ref[here], du_ref[here], ((0,), (0,)))
            down_acc[...] += mm(dy_ref[here], m_ref[here], ((0,), (0,)))
            return carry

        lax.fori_loop(0, tiles, tile, 0)
    up_out[0] = up_acc[...].astype(jnp.bfloat16)
    down_out[0] = down_acc[...].astype(jnp.bfloat16)


def weight_grads(plans, saved, experts, plan_row):
    halves = len(plans)
    flat = [array for group in saved for array in group]
    width, hidden = flat[0].shape[1], flat[1].shape[1]
    block = pl.BlockSpec((1, width, hidden), lambda e, *p: (e, 0, 0))
    shape = jax.ShapeDtypeStruct((experts, width, hidden), jnp.bfloat16)
    return pl.pallas_call(
        functools.partial(grads_kernel, halves=halves, plan_row=plan_row),
        grid_spec=pltpu.PrefetchScalarGridSpec(
            num_scalar_prefetch=halves,
            grid=(experts,),
            in_specs=[pl.BlockSpec(memory_space=pltpu.VMEM)] * len(flat),
            out_specs=[block, block],
            scratch_shapes=[pltpu.VMEM((width, hidden), jnp.float32)] * 2,
        ),
        out_shape=[shape, shape],
        compiler_params=pltpu.CompilerParams(vmem_limit_bytes=56 * 2**20),
        cost_estimate=pl.CostEstimate(flops=8 * 2048 * width * hidden, bytes_accessed=30 * 2**20, transcendentals=0),
        name="expert_weight_grads",
    )(*plans, *flat)


EPS = 1e-06
F32 = jnp.float32
BF16 = jnp.bfloat16


def norm_rows(values, gain_vector):
    return values * lax.rsqrt(jnp.mean(values * values, axis=-1, keepdims=True) + EPS) * gain_vector


def swap(values, axis, bit):
    count = lax.axis_size(axis)
    return lax.ppermute(values, axis, [(i, i ^ bit) for i in range(count)])


def gather_shares(mine):
    far = swap(mine, "tensor", 2)
    near = swap(mine, "tensor", 1)
    return jnp.concatenate([mine, near]), jnp.concatenate([far, swap(far, "tensor", 1)])


def sum_shares(for_me, for_near, for_far, for_both):
    passed = swap(for_both.astype(BF16), "tensor", 1).astype(F32)
    far = swap((for_far + passed).astype(BF16), "tensor", 2).astype(F32)
    near = swap(for_near.astype(BF16), "tensor", 1).astype(F32)
    return for_me + near + far


def scatter_sum(values):
    count = lax.axis_size("dp")
    index = lax.axis_index("dp")
    experts, rows, width = values.shape
    piece = rows // count
    bit = 1
    while bit < count:
        values = values.reshape(experts, count // (2 * bit), 2, piece, width)
        mine = (index // bit) % 2
        keep = lax.dynamic_index_in_dim(values, mine, 2, keepdims=False)
        send = lax.dynamic_index_in_dim(values, 1 - mine, 2, keepdims=False)
        values = keep.astype(F32) + swap(send.astype(BF16), "dp", bit).astype(F32)
        bit *= 2
    return values.reshape(experts, piece, width)


def sum_everywhere(values):
    for axis in ("tensor", "dp"):
        bit = 1
        while bit < lax.axis_size(axis):
            values = values + swap(values, axis, bit)
            bit *= 2
    return values


def on_device(
    tokens,
    attn_gain,
    qkv_weight,
    proj_weight,
    bias_table,
    buckets,
    ffn_gain,
    router_weight,
    routes,
    up_weight,
    down_weight,
    cotangent,
):
    highest = lax.Precision.HIGHEST
    rank = lax.axis_index("tensor")
    core, chip = rank % 2, rank // 2
    tensor_count = lax.axis_size("tensor")
    rows, width = tokens.shape
    share = rows // tensor_count
    half = rows // 2
    seq_len = (buckets.shape[0] + 1) // 2
    heads, bucket_count = bias_table.shape
    experts = up_weight.shape[0]
    own_seq = chip.astype(jnp.int32).reshape(1)
    other_seq = 1 - own_seq

    flipped = buckets[::-1]
    cut = KB - 1
    turned = jnp.concatenate([flipped[cut:], jnp.full((1,), -1, flipped.dtype), flipped[:cut]])
    bucket_hot = (turned[:, None] == jnp.arange(bucket_count)[None, :]).astype(F32)
    offsets = jnp.dot(bias_table, bucket_hot.T, precision=highest)[:, None, :]

    all_routes = routes[:, 0].reshape(tensor_count, share)
    counts = jnp.sum((all_routes[:, :, None] == jnp.arange(experts)).astype(jnp.int32), axis=1)
    order = rank ^ jnp.arange(tensor_count)
    same = order[:, None] == jnp.arange(tensor_count)[None, :]
    counts = jnp.sum(jnp.where(same[:, :, None], counts[None], 0), axis=1)
    own_plan = plan_segments(counts[:2])
    other_plan = plan_segments(counts[2:])
    my_routes = lax.dynamic_slice_in_dim(routes[:, 0], rank * share, share, 0)
    my_hot = (my_routes[:, None] == jnp.arange(experts)[None, :]).astype(F32)
    earlier = (jnp.arange(share)[:, None] > jnp.arange(share)[None, :]).astype(BF16)
    ahead = jnp.dot(earlier, my_hot.astype(BF16), preferred_element_type=F32)
    starts = (jnp.cumsum(counts[0]) - counts[0]).astype(F32)
    position = jnp.sum(my_hot * (ahead + starts[None, :]), axis=1).astype(jnp.int32)
    place = jnp.arange(share)[:, None] == position[None, :]
    place_matrix = place.astype(BF16)

    def sort_rows(values):
        return jnp.dot(place_matrix, values, preferred_element_type=F32).astype(BF16)

    def unsort_rows(values):
        dims = (((0,), (0,)), ((), ()))
        high = lax.reduce_precision(values, 8, 7)
        low = (values - high).astype(BF16)
        return lax.dot_general(
            place_matrix, high.astype(BF16), dims, preferred_element_type=F32
        ) + lax.dot_general(place_matrix, low, dims, preferred_element_type=F32)

    own_grad_out, other_grad_out = gather_shares(sort_rows(cotangent))

    normed_one = norm_rows(tokens.astype(F32), attn_gain).astype(BF16)
    input_share = lax.dynamic_slice_in_dim(tokens, rank * share, share, 0).astype(F32)
    qkv = jnp.einsum("cdf,td->cft", qkv_weight, normed_one, preferred_element_type=F32).astype(BF16)

    def columns(values, core_index):
        return lax.dynamic_slice_in_dim(values, core_index * share, share, values.ndim - 1)

    def project(mixed, core_index):
        return jnp.einsum(
            "ft,df->td", columns(mixed, core_index), proj_weight, preferred_element_type=F32
        )

    mixed_other, lse_other = forward_attention(other_seq, qkv, offsets, seq_len)
    mixed_own, lse_own = forward_attention(own_seq, qkv, offsets, seq_len)
    attn_share = sum_shares(
        project(mixed_own, core),
        project(mixed_own, 1 - core),
        project(mixed_other, core),
        project(mixed_other, 1 - core),
    )
    hidden_share = input_share + attn_share
    normed_two = norm_rows(hidden_share, ffn_gain).astype(BF16)

    own_rows, other_rows = gather_shares(sort_rows(normed_two))
    padded_router = jnp.pad(router_weight, ((0, 0), (0, 128 - experts)))
    own_out, own_back, own_gate, *own_saved = run_experts(
        own_plan, own_rows, own_grad_out, padded_router, up_weight, down_weight, 2
    )
    other_out, other_back, other_gate, *other_saved = run_experts(
        other_plan, other_rows, other_grad_out, padded_router, up_weight, down_weight, 2
    )
    back_share = unsort_rows(
        sum_shares(own_back[:share], own_back[share:], other_back[:share], other_back[share:])
    )
    passed = swap(other_gate[share:, 0], "tensor", 1)
    gate_sorted = (
        own_gate[:share, 0]
        + swap(own_gate[share:, 0], "tensor", 1)
        + swap(other_gate[:share, 0] + passed, "tensor", 2)
    )
    gate_grad = jnp.sum(jnp.where(place, gate_sorted[:, None], 0.0), axis=0)
    up_grad, down_grad = weight_grads(
        [own_plan, other_plan], [own_saved, other_saved], experts, 8
    )

    logits = jnp.dot(normed_two, router_weight, preferred_element_type=F32)
    router_probs = jax.nn.softmax(logits, axis=-1)
    gate_prob = jnp.sum(router_probs * my_hot, axis=-1)
    grad_out = cotangent.astype(F32)
    logit_grad = ((gate_grad * gate_prob)[:, None] * (my_hot - router_probs)).astype(BF16)
    router_grad = jnp.einsum("td,te->de", normed_two, logit_grad, preferred_element_type=F32)
    normed_grad = back_share + jnp.einsum(
        "te,de->td", logit_grad, router_weight, preferred_element_type=F32
    )
    hidden_part, ffn_gain_grad = jax.vjp(norm_rows, hidden_share, ffn_gain)[1](normed_grad)
    hidden_grad = grad_out + hidden_part

    attn_grad = hidden_grad.astype(BF16)
    far_grad = swap(attn_grad, "tensor", 2)
    near_grad = swap(attn_grad, "tensor", 1)
    both_grad = swap(far_grad, "tensor", 1)

    def in_order(mine, partner):
        return jnp.concatenate(
            [jnp.where(core == 0, mine, partner), jnp.where(core == 0, partner, mine)]
        )

    own_attn_grad = in_order(attn_grad, near_grad)
    other_attn_grad = in_order(far_grad, both_grad)

    def mixed_grad(rows_grad):
        return jnp.einsum("df,td->ft", proj_weight, rows_grad, preferred_element_type=F32).astype(
            BF16
        )

    own_qkv_grad, own_diag = backward_attention(
        own_seq, qkv, mixed_grad(own_attn_grad), lse_own, offsets, seq_len
    )
    other_qkv_grad, other_diag = backward_attention(
        other_seq, qkv, mixed_grad(other_attn_grad), lse_other, offsets, seq_len
    )

    def input_part(qkv_rows, core_index):
        return jnp.einsum(
            "cft,cdf->td", columns(qkv_rows, core_index), qkv_weight, preferred_element_type=F32
        )

    input_share_grad = sum_shares(
        input_part(own_qkv_grad, core),
        input_part(own_qkv_grad, 1 - core),
        input_part(other_qkv_grad, core),
        input_part(other_qkv_grad, 1 - core),
    )
    own_normed = lax.dynamic_slice_in_dim(normed_one, chip * half, half, 0)
    other_normed = lax.dynamic_slice_in_dim(normed_one, (1 - chip) * half, half, 0)
    qkv_grad = jnp.einsum(
        "td,cft->cdf", own_normed, own_qkv_grad, preferred_element_type=F32
    ) + jnp.einsum("td,cft->cdf", other_normed, other_qkv_grad, preferred_element_type=F32)
    proj_grad = jnp.einsum(
        "td,ft->df", own_attn_grad, mixed_own, preferred_element_type=F32
    ) + jnp.einsum("td,ft->df", other_attn_grad, mixed_other, preferred_element_type=F32)
    token_part = jax.vjp(lambda rows_in: norm_rows(rows_in, attn_gain), input_share)[1](
        input_share_grad
    )[0]
    tokens_grad = hidden_grad + token_part
    attn_gain_grad = jnp.sum(qkv_weight.astype(F32) * qkv_grad, axis=(0, 2)) / attn_gain

    expert_share = unsort_rows(
        sum_shares(own_out[:share], own_out[share:], other_out[:share], other_out[share:])
    )
    layer_out = (hidden_share + gate_prob[:, None] * expert_share).astype(BF16)

    table_local = jnp.dot((own_diag + other_diag)[:, 0], bucket_hot, precision=highest)
    table_full = lax.dynamic_update_slice_in_dim(
        jnp.zeros((heads * tensor_count, bucket_count), F32), table_local, rank * heads, 0
    )
    small = [attn_gain_grad, ffn_gain_grad, router_grad.reshape(-1), table_full.reshape(-1)]
    sizes = [array.size for array in small]
    packed = jnp.concatenate(small)
    packed = jnp.pad(packed, (0, -packed.size % 1024)).reshape(-1, 128)
    packed = sum_everywhere(packed).reshape(-1)
    ends = [sum(sizes[:i]) for i in range(5)]
    attn_gain_grad, ffn_gain_grad, router_grad, table_grad = [
        packed[ends[i] : ends[i + 1]] for i in range(4)
    ]
    split = experts // 2
    down_grad = jnp.concatenate([scatter_sum(down_grad[:split]), scatter_sum(down_grad[split:])])
    up_grad = jnp.concatenate([scatter_sum(up_grad[:split]), scatter_sum(up_grad[split:])])
    return (
        layer_out,
        tokens_grad,
        attn_gain_grad,
        scatter_sum(qkv_grad),
        scatter_sum(proj_grad[None])[0],
        table_grad.reshape(heads * tensor_count, bucket_count),
        ffn_gain_grad,
        router_grad.reshape(router_weight.shape),
        up_grad,
        down_grad,
    )


def solution(mesh):
    placed = (
        P("dp", None),
        P(),
        P(None, None, "tensor"),
        P(None, "tensor"),
        P("tensor", None),
        P(),
        P(),
        P(),
        P("dp", None),
        P(None, None, "tensor"),
        P(None, None, "tensor"),
        P(("dp", "tensor"), None),
    )
    return jax.shard_map(
        on_device,
        mesh=mesh,
        in_specs=placed,
        out_specs=(
            P(("dp", "tensor"), None),
            P(("dp", "tensor"), None),
            P(),
            P(None, "dp", "tensor"),
            P("dp", "tensor"),
            P(),
            P(),
            P(),
            P(None, "dp", "tensor"),
            P(None, "dp", "tensor"),
        ),
        check_vma=False,
    )
```

```python
import functools
import jax, jax.numpy as jnp
from jax import lax
from jax.experimental import pallas as pl
from jax.experimental.pallas import tpu as pltpu
from jax.sharding import PartitionSpec as P

QB = 256
KB = 128


def mm(a, b, dims):
    return lax.dot_general(a, b, (dims, ((), ())), preferred_element_type=jnp.float32)


def score_block(keys, queries, skew, first_query, seq_len):
    scores = mm(keys, queries, ((1,), (0,)))
    bias = [
        skew[:, pl.ds(pl.multiple_of(first_query - first_key + seq_len - KB, KB), QB)]
        for first_key in range(0, seq_len, KB)
    ]
    return scores + jnp.concatenate(bias, axis=0)


def forward_kernel(seq_ref, qkv_ref, offset_ref, mixed_ref, lse_ref, skew):
    seq_len = qkv_ref.shape[2]
    scale = qkv_ref.shape[1] ** -0.5
    skew[...] = pltpu.roll(
        jnp.broadcast_to(offset_ref[0], (KB, 2 * seq_len)), 0, 1, stride=1, stride_axis=0
    )
    keys = qkv_ref[1].T
    values = qkv_ref[2]

    def block(index, carry):
        first = pl.multiple_of(index * QB, QB)
        queries = qkv_ref[0, :, pl.ds(first, QB)] * jnp.bfloat16(scale)
        scores = score_block(keys, queries, skew, first, seq_len)
        largest = jnp.max(scores, axis=0, keepdims=True)
        expos = jnp.exp(scores - largest)
        total = jnp.sum(expos, axis=0, keepdims=True)
        weights = (expos * (1.0 / total)).astype(jnp.bfloat16)
        mixed_ref[:, pl.ds(first, QB)] = mm(values, weights, ((1,), (0,))).astype(jnp.bfloat16)
        lse_ref[0, :, pl.ds(first, QB)] = largest + jnp.log(total)
        return carry

    lax.fori_loop(0, seq_len // QB, block, 0, unroll=True)


def forward_attention(seq, qkv, offsets, seq_len):
    _, width, rows = qkv.shape
    heads = offsets.shape[0]
    size = width // heads
    return pl.pallas_call(
        forward_kernel,
        grid_spec=pltpu.PrefetchScalarGridSpec(
            num_scalar_prefetch=1,
            grid=(heads,),
            in_specs=[
                pl.BlockSpec((3, size, seq_len), lambda h, s: (0, h, s[0])),
                pl.BlockSpec((1, 1, 2 * seq_len), lambda h, s: (h, 0, 0)),
            ],
            out_specs=[
                pl.BlockSpec((size, seq_len), lambda h, s: (h, 0)),
                pl.BlockSpec((1, 1, seq_len), lambda h, s: (h, 0, 0)),
            ],
            scratch_shapes=[pltpu.VMEM((KB, 2 * seq_len), jnp.float32)],
        ),
        out_shape=[
            jax.ShapeDtypeStruct((width, seq_len), jnp.bfloat16),
            jax.ShapeDtypeStruct((heads, 1, seq_len), jnp.float32),
        ],
        compiler_params=pltpu.CompilerParams(vmem_limit_bytes=48 * 2**20),
        cost_estimate=pl.CostEstimate(
            flops=60 * heads * seq_len * seq_len * size,
            bytes_accessed=30 * 2**20,
            transcendentals=heads * seq_len * seq_len,
        ),
        name="attention_forward",
    )(seq, qkv, offsets)


def backward_kernel(
    seq_ref, qkv_ref, grad_ref, lse_ref, offset_ref, out_ref, diag_ref, skew, sums, probs_all, score_all
):
    seq_len = qkv_ref.shape[2]
    scale = qkv_ref.shape[1] ** -0.5
    skew[...] = pltpu.roll(
        jnp.broadcast_to(offset_ref[0], (KB, 2 * seq_len)), 0, 1, stride=1, stride_axis=0
    )
    sums[...] = jnp.zeros_like(sums)
    keys_t = qkv_ref[1]
    keys = keys_t.T
    values = qkv_ref[2].T

    def block(index, carry):
        first = pl.multiple_of(index * QB, QB)
        here = pl.ds(first, QB)
        queries = qkv_ref[0, :, here] * jnp.bfloat16(scale)
        scores = score_block(keys, queries, skew, first, seq_len)
        probs = jnp.exp(scores - lse_ref[0, :, here])
        probs_all[:, here] = probs.astype(jnp.bfloat16)
        prob_grad = mm(values, grad_ref[:, here], ((1,), (0,)))
        centre = jnp.sum(probs * prob_grad, axis=0, keepdims=True)
        score_grad = probs * (prob_grad - centre)
        rounded = score_grad.astype(jnp.bfloat16)
        score_all[:, here] = rounded
        for first_key in range(0, seq_len, KB):
            spot = pl.ds(pl.multiple_of(first - first_key + seq_len - KB, KB), QB)
            sums[:, spot] += score_grad[first_key : first_key + KB]
        out_ref[0, :, here] = (mm(keys_t, rounded, ((1,), (0,))) * scale).astype(jnp.bfloat16)
        return carry

    lax.fori_loop(0, seq_len // QB, block, 0, unroll=True)
    queries = qkv_ref[0] * jnp.bfloat16(scale)
    out_ref[1] = mm(queries, score_all[...], ((1,), (1,))).astype(jnp.bfloat16)
    out_ref[2] = mm(grad_ref[...], probs_all[...], ((1,), (1,))).astype(jnp.bfloat16)
    part = sums[...]
    half = KB // 2
    while half >= 1:
        part = part[:half] + pltpu.roll(part[half:], 2 * seq_len - half, 1)
        half //= 2
    diag_ref[0] = part


def backward_attention(seq, qkv, grads, lse, offsets, seq_len):
    _, width, rows = qkv.shape
    heads = offsets.shape[0]
    size = width // heads
    return pl.pallas_call(
        backward_kernel,
        grid_spec=pltpu.PrefetchScalarGridSpec(
            num_scalar_prefetch=1,
            grid=(heads,),
            in_specs=[
                pl.BlockSpec((3, size, seq_len), lambda h, s: (0, h, s[0])),
                pl.BlockSpec((size, seq_len), lambda h, s: (h, 0)),
                pl.BlockSpec((1, 1, seq_len), lambda h, s: (h, 0, 0)),
                pl.BlockSpec((1, 1, 2 * seq_len), lambda h, s: (h, 0, 0)),
            ],
            out_specs=[
                pl.BlockSpec((3, size, seq_len), lambda h, s: (0, h, 0)),
                pl.BlockSpec((1, 1, 2 * seq_len), lambda h, s: (h, 0, 0)),
            ],
            scratch_shapes=[
                pltpu.VMEM((KB, 2 * seq_len), jnp.float32),
                pltpu.VMEM((KB, 2 * seq_len), jnp.float32),
                pltpu.VMEM((seq_len, seq_len), jnp.bfloat16),
                pltpu.VMEM((seq_len, seq_len), jnp.bfloat16),
            ],
        ),
        out_shape=[
            jax.ShapeDtypeStruct((3, width, seq_len), jnp.bfloat16),
            jax.ShapeDtypeStruct((heads, 1, 2 * seq_len), jnp.float32),
        ],
        compiler_params=pltpu.CompilerParams(vmem_limit_bytes=48 * 2**20),
        cost_estimate=pl.CostEstimate(
            flops=70 * heads * seq_len * seq_len * size,
            bytes_accessed=40 * 2**20,
            transcendentals=heads * seq_len * seq_len,
        ),
        name="attention_backward",
    )(seq, qkv, grads, lse, offsets)


CH = 16
UNIT = 128
FIELDS = 4


def unit_limit(rows, shares, experts):
    chunks = rows // CH + shares * (experts - 1)
    return (chunks + experts * (UNIT // CH - 1)) // (UNIT // CH)


def plan_segments(counts):
    starts = jnp.cumsum(counts, axis=1) - counts
    first = starts // CH
    chunks = jnp.where(counts > 0, (starts + counts + CH - 1) // CH - first, 0)
    units = (jnp.sum(chunks, axis=0) * CH + UNIT - 1) // UNIT
    base = jnp.cumsum(units) - units
    return jnp.concatenate(
        [first, chunks, starts, starts + counts, units[None], base[None]], axis=0
    ).astype(jnp.int32)


def for_units(units, step):
    def double(index, carry):
        step(index * (2 * UNIT), 2 * UNIT)
        return carry

    lax.fori_loop(0, units // 2, double, 0)

    @pl.when(units % 2 == 1)
    def _():
        step((units - 1) * UNIT, UNIT)


def at_rows(start, size):
    return pl.ds(pl.multiple_of(start, size if size < UNIT else UNIT), size)


def gather_rows(plan_ref, expert, shares, units, rows_refs, grad_refs, xs, cs, base):
    filled = 0
    for share in range(shares):
        first = plan_ref[share, expert]
        chunks = plan_ref[shares + share, expert]
        start = plan_ref[2 * shares + share, expert]
        end = plan_ref[3 * shares + share, expert]
        x_ref, c_ref = rows_refs[share], grad_refs[share]

        def gather(index, carry):
            here = (first + index) * CH
            local = (filled + index) * CH
            row = here + lax.broadcasted_iota(jnp.int32, (CH, 1), 0)
            keep = (row >= start) & (row < end)
            zero = jnp.zeros((), jnp.bfloat16)
            xs[at_rows(base + local, CH)] = jnp.where(keep, x_ref[at_rows(here, CH)], zero)
            cs[at_rows(local, CH)] = jnp.where(keep, c_ref[at_rows(here, CH)], zero)
            return carry

        lax.fori_loop(0, chunks, gather, 0)
        filled = filled + chunks

    def clear(index, carry):
        xs[at_rows(base + index * CH, CH)] = jnp.zeros((CH, xs.shape[1]), jnp.bfloat16)
        cs[at_rows(index * CH, CH)] = jnp.zeros((CH, cs.shape[1]), jnp.bfloat16)
        return carry

    lax.fori_loop(filled, units * (UNIT // CH), clear, 0)


def scatter_rows(plan_ref, expert, shares, buffers, outs):
    filled = 0
    for share in range(shares):
        first = plan_ref[share, expert]
        chunks = plan_ref[shares + share, expert]

        def scatter(index, carry):
            target = at_rows((first + index) * CH, CH)
            local = at_rows((filled + index) * CH, CH)
            for buffer, targets in zip(buffers, outs):
                out = targets[share]
                out[target] = (out[target].astype(jnp.float32) + buffer[local]).astype(out.dtype)
            return carry

        lax.fori_loop(0, chunks, scatter, 0)
        filled = filled + chunks


def expert_kernel(*refs, shares, first_expert, expert_count, with_grads):
    plan_ref, refs = refs[0], refs[1:]
    if with_grads:
        past_plan, refs = refs[0], refs[1:]
    x_refs, refs = refs[:shares], refs[shares:]
    c_refs, refs = refs[:shares], refs[shares:]
    router_ref, up_ref, down_ref, *refs = refs
    if with_grads:
        past, refs = refs[:4], refs[4:]
    y_refs, refs = refs[:shares], refs[shares:]
    back_refs, refs = refs[:shares], refs[shares:]
    gate_refs, refs = refs[:shares], refs[shares:]
    if with_grads:
        up_out, down_out, *refs = refs
        xs, ms, dys, dus, cs, ybuf, bbuf, gbuf, *refs = refs
        old, up_acc, down_acc, sems = refs[:4], refs[4], refs[5], refs[6]
    else:
        xs, ms, dys, dus, cs, ybuf, bbuf, gbuf = refs
    step = pl.program_id(0)
    expert = step + first_expert
    units = plan_ref[4 * shares, expert]
    base = 0 if with_grads else plan_ref[4 * shares + 1, expert] * UNIT

    @pl.when(step == 0)
    def _():
        for out in (*y_refs, *back_refs, *gate_refs):
            out[...] = jnp.zeros_like(out)

    if with_grads:
        past_units = past_plan[4 * shares, expert]
        past_base = past_plan[4 * shares + 1, expert] * UNIT

        def copies(index):
            return [
                pltpu.make_async_copy(
                    source.at[at_rows(past_base + index * UNIT, UNIT)],
                    target.at[at_rows(index * UNIT, UNIT)],
                    sems.at[which, index],
                )
                for which, (source, target) in enumerate(zip(past, old))
            ]

        def begin(index, carry):
            for copy in copies(index):
                copy.start()
            return carry

        def finish(index, carry):
            for copy in copies(index):
                copy.wait()
            return carry

        lax.fori_loop(0, past_units, begin, 0)

    gather_rows(plan_ref, expert, shares, units, x_refs, c_refs, xs, cs, base)

    def tile(start, size):
        local = at_rows(start, size)
        saved = at_rows(base + start, size)
        x = xs[saved]
        c = cs[local].astype(jnp.float32)
        logits = mm(x, router_ref[...], ((1,), (0,)))
        lane = lax.broadcasted_iota(jnp.int32, logits.shape, 1)
        logits = jnp.where(lane < expert_count, logits, -jnp.inf)
        expos = jnp.exp(logits - jnp.max(logits, axis=1, keepdims=True))
        mine = jnp.sum(jnp.where(lane == expert, expos, 0.0), axis=1, keepdims=True)
        gate = mine / jnp.sum(expos, axis=1, keepdims=True)
        dy = (gate * c).astype(jnp.bfloat16)
        dys[saved] = dy
        u = mm(x, up_ref[0], ((1,), (0,)))
        dm = mm(dy, down_ref[0], ((1,), (0,)))
        root = 0.7978845608028654
        square = u * u
        bent = jnp.tanh(root * (u * (1.0 + 0.044715 * square)))
        half = 0.5 * (1.0 + bent)
        m = (u * half).astype(jnp.bfloat16)
        ms[saved] = m
        slope = half + (0.5 * root) * (u * ((1.0 - bent * bent) * (1.0 + (3 * 0.044715) * square)))
        du = (slope * dm).astype(jnp.bfloat16)
        dus[saved] = du
        y = mm(m, down_ref[0], ((1,), (1,)))
        ybuf[local] = y
        gbuf[local] = jnp.broadcast_to(jnp.sum(y * c, axis=1, keepdims=True), (size, gbuf.shape[1]))
        bbuf[local] = mm(du, up_ref[0], ((1,), (1,)))

    for_units(units, tile)
    scatter_rows(
        plan_ref, expert, shares, (ybuf, bbuf, gbuf), (y_refs, back_refs, gate_refs)
    )

    if with_grads:
        up_acc[...] = jnp.zeros_like(up_acc)
        down_acc[...] = jnp.zeros_like(down_acc)

        def add(arrays):
            def part(start, size):
                here = at_rows(start, size)
                x, m, dy, du = [array[here] for array in arrays]
                up_acc[...] += mm(x, du, ((0,), (0,)))
                down_acc[...] += mm(dy, m, ((0,), (0,)))

            return part

        for_units(units, add((xs, ms, dys, dus)))
        lax.fori_loop(0, past_units, finish, 0)
        for_units(past_units, add(old))
        up_out[0] = up_acc[...].astype(jnp.bfloat16)
        down_out[0] = down_acc[...].astype(jnp.bfloat16)


def run_experts(plan, x, c, router, up, down, past=None, first_expert=0, step_count=None):
    shares = len(x)
    rows, width = x[0].shape
    experts, _, hidden = up.shape
    steps = step_count or experts
    with_grads = past is not None
    saved = unit_limit(rows * shares, shares, experts) * UNIT
    most = rows * shares
    brain, full = jnp.bfloat16, jnp.float32
    whole = lambda shape: pl.BlockSpec(shape, lambda e, *p: (0, 0))
    block = pl.BlockSpec((1, width, hidden), lambda e, *p: (first_expert + e, 0, 0))
    scalars = [plan]
    inputs = [*x, *c, router, up, down]
    in_specs = [whole((rows, width))] * (2 * shares) + [whole(router.shape), block, block]
    row_types = [full] + [brain] * (shares - 1)
    out_shape = [jax.ShapeDtypeStruct((rows, width), kind) for kind in row_types * 2]
    out_specs = [whole((rows, width))] * (2 * shares) + [whole((rows, 128))] * shares
    out_shape += [jax.ShapeDtypeStruct((rows, 128), full)] * shares
    scratch = [
        pltpu.VMEM((most, width), brain),
        pltpu.VMEM((most, width), full),
        pltpu.VMEM((most, width), full),
        pltpu.VMEM((most, 128), full),
    ]
    widths = (width, hidden, width, hidden)
    if with_grads:
        past_plan, past_arrays = past
        scalars.append(past_plan)
        inputs += past_arrays
        in_specs += [pl.BlockSpec(memory_space=pl.ANY)] * 4
        grad_block = pl.BlockSpec((1, width, hidden), lambda e, *p: (e, 0, 0))
        out_specs += [grad_block, grad_block]
        out_shape += [jax.ShapeDtypeStruct((steps, width, hidden), brain)] * 2
        buffers = [pltpu.VMEM((most, size), brain) for size in widths]
        scratch = (
            buffers
            + scratch
            + buffers
            + [pltpu.VMEM((width, hidden), full)] * 2
            + [pltpu.SemaphoreType.DMA((4, most // UNIT))]
        )
    else:
        out_specs += [whole((saved, size)) for size in widths]
        out_shape += [jax.ShapeDtypeStruct((saved, size), brain) for size in widths]
    return pl.pallas_call(
        functools.partial(
            expert_kernel,
            shares=shares,
            first_expert=first_expert,
            expert_count=experts,
            with_grads=with_grads,
        ),
        grid_spec=pltpu.PrefetchScalarGridSpec(
            num_scalar_prefetch=len(scalars),
            grid=(steps,),
            in_specs=in_specs,
            out_specs=out_specs,
            scratch_shapes=scratch,
        ),
        out_shape=out_shape,
        compiler_params=pltpu.CompilerParams(vmem_limit_bytes=58 * 2**20),
        cost_estimate=pl.CostEstimate(
            flops=20 * rows * shares * width * hidden * steps // experts,
            bytes_accessed=30 * 2**20,
            transcendentals=0,
        ),
        name="experts_and_grads" if with_grads else "experts",
    )(*scalars, *inputs)


EPS = 1e-06
F32 = jnp.float32
BF16 = jnp.bfloat16


def norm_rows(values, gain_vector):
    return values * lax.rsqrt(jnp.mean(values * values, axis=-1, keepdims=True) + EPS) * gain_vector


def swap(values, axis, bit):
    count = lax.axis_size(axis)
    return lax.ppermute(values, axis, [(i, i ^ bit) for i in range(count)])


def after(value, *milestones):
    return lax.optimization_barrier((value, milestones))[0]


class ScatterSum:
    def __init__(self, values):
        self.values = values
        self.bit = 1
        self.count = lax.axis_size("dp")
        self.piece = values.shape[1] // self.count
        self.moving = None

    def start(self, *milestones):
        if self.moving is not None:
            keep, received = after((self.keep, self.moving), *milestones)
            self.values = keep.astype(F32) + received.astype(F32)
            self.moving = None
        if self.bit >= self.count:
            return
        experts, width = self.values.shape[0], self.values.shape[-1]
        shape = (experts, self.count // (2 * self.bit), 2, self.piece, width)
        values = after(self.values, *milestones).reshape(shape)
        mine = (lax.axis_index("dp") // self.bit) % 2
        self.keep = lax.dynamic_index_in_dim(values, mine, 2, keepdims=False)
        send = lax.dynamic_index_in_dim(values, 1 - mine, 2, keepdims=False)
        self.sent = send.astype(BF16)
        self.moving = swap(self.sent, "dp", self.bit)
        self.bit *= 2

    def finish(self):
        while self.moving is not None or self.bit < self.count:
            self.start()
        return self.values.reshape(self.values.shape[0], self.piece, self.values.shape[-1])


def sum_everywhere(values):
    for axis in ("tensor", "dp"):
        bit = 1
        while bit < lax.axis_size(axis):
            values = values + swap(values, axis, bit)
            bit *= 2
    return values


def on_device(
    tokens,
    attn_gain,
    qkv_weight,
    proj_weight,
    bias_table,
    buckets,
    ffn_gain,
    router_weight,
    routes,
    up_weight,
    down_weight,
    cotangent,
):
    highest = lax.Precision.HIGHEST
    rank = lax.axis_index("tensor")
    core, chip = rank % 2, rank // 2
    tensor_count = lax.axis_size("tensor")
    rows, width = tokens.shape
    share = rows // tensor_count
    half = rows // 2
    seq_len = (buckets.shape[0] + 1) // 2
    heads, bucket_count = bias_table.shape
    experts = up_weight.shape[0]
    own_seq = chip.astype(jnp.int32).reshape(1)
    other_seq = 1 - own_seq

    flipped = buckets[::-1]
    cut = KB - 1
    turned = jnp.concatenate([flipped[cut:], jnp.full((1,), -1, flipped.dtype), flipped[:cut]])
    bucket_hot = (turned[:, None] == jnp.arange(bucket_count)[None, :]).astype(F32)
    offsets = jnp.dot(bias_table, bucket_hot.T, precision=highest)[:, None, :]

    all_routes = routes[:, 0].reshape(tensor_count, share)
    counts = jnp.sum((all_routes[:, :, None] == jnp.arange(experts)).astype(jnp.int32), axis=1)
    order = rank ^ jnp.arange(tensor_count)
    same = order[:, None] == jnp.arange(tensor_count)[None, :]
    counts = jnp.sum(jnp.where(same[:, :, None], counts[None], 0), axis=1)
    own_plan = plan_segments(counts[:2])
    other_plan = plan_segments(counts[2:])
    my_routes = lax.dynamic_slice_in_dim(routes[:, 0], rank * share, share, 0)
    my_hot = (my_routes[:, None] == jnp.arange(experts)[None, :]).astype(F32)
    earlier = (jnp.arange(share)[:, None] > jnp.arange(share)[None, :]).astype(BF16)
    ahead = jnp.dot(earlier, my_hot.astype(BF16), preferred_element_type=F32)
    starts = (jnp.cumsum(counts[0]) - counts[0]).astype(F32)
    position = jnp.sum(my_hot * (ahead + starts[None, :]), axis=1).astype(jnp.int32)
    place = jnp.arange(share)[:, None] == position[None, :]
    place_matrix = place.astype(BF16)

    def sort_rows(values):
        return jnp.dot(place_matrix, values, preferred_element_type=F32).astype(BF16)

    def unsort_rows(values):
        dims = (((0,), (0,)), ((), ()))
        high = lax.reduce_precision(values, 8, 7)
        low = (values - high).astype(BF16)
        return lax.dot_general(
            place_matrix, high.astype(BF16), dims, preferred_element_type=F32
        ) + lax.dot_general(place_matrix, low, dims, preferred_element_type=F32)

    grad_mine = sort_rows(cotangent)
    grad_far = swap(grad_mine, "tensor", 2)
    grad_near = swap(grad_mine, "tensor", 1)

    normed_one = norm_rows(tokens.astype(F32), attn_gain).astype(BF16)
    input_share = lax.dynamic_slice_in_dim(tokens, rank * share, share, 0).astype(F32)
    qkv = jnp.einsum("cdf,td->cft", qkv_weight, normed_one, preferred_element_type=F32).astype(BF16)

    def columns(values, core_index):
        return lax.dynamic_slice_in_dim(values, core_index * share, share, values.ndim - 1)

    def project(mixed, core_index):
        return jnp.einsum(
            "ft,df->td", columns(mixed, core_index), proj_weight, preferred_element_type=F32
        )

    mixed_other, lse_other = forward_attention(other_seq, qkv, offsets, seq_len)
    passed = swap(project(mixed_other, 1 - core).astype(BF16), "tensor", 1)
    attn_sent = (project(mixed_other, core) + passed.astype(F32)).astype(BF16)
    attn_far = swap(attn_sent, "tensor", 2)
    mixed_own, lse_own = forward_attention(after(own_seq, attn_sent), qkv, offsets, seq_len)
    attn_near = swap(project(mixed_own, 1 - core).astype(BF16), "tensor", 1)
    attn_share = project(mixed_own, core) + attn_near.astype(F32) + attn_far.astype(F32)
    grad_far = after(grad_far, mixed_own)
    grad_both = swap(grad_far, "tensor", 1)
    hidden_share = input_share + attn_share
    normed_two = norm_rows(hidden_share, ffn_gain).astype(BF16)

    rows_mine = sort_rows(normed_two)
    rows_far = swap(rows_mine, "tensor", 2)
    rows_near = swap(rows_mine, "tensor", 1)
    padded_router = jnp.pad(router_weight, ((0, 0), (0, 128 - experts)))
    own = run_experts(
        own_plan, [rows_mine, rows_near], [grad_mine, grad_near], padded_router, up_weight, down_weight
    )
    past = (own_plan, own[6:])
    rows_far = after(rows_far, own[0])
    other_rows = [rows_far, swap(rows_far, "tensor", 1)]
    split = experts // 2

    def run_other(plan, start):
        return run_experts(
            plan, other_rows, [grad_far, grad_both], padded_router, up_weight, down_weight,
            past, start, split,
        )

    first = run_other(other_plan, 0)
    down_one, up_one = ScatterSum(first[7]), ScatterSum(first[6])
    down_one.start()
    second = run_other(after(other_plan, down_one.sent), split)
    down_two, up_two = ScatterSum(second[7]), ScatterSum(second[6])
    other = [one.astype(F32) + two.astype(F32) for one, two in zip(first[:6], second[:6])]
    back_passed = swap(other[3].astype(BF16), "tensor", 1)
    passed = swap(other[5][:, 0], "tensor", 1)
    back_sent = (other[2] + back_passed.astype(F32)).astype(BF16)
    back_far = swap(back_sent, "tensor", 2)
    gate_sorted = (
        own[4][:, 0]
        + swap(own[5][:, 0], "tensor", 1)
        + swap(other[4][:, 0] + passed, "tensor", 2)
    )
    back_near = swap(own[3], "tensor", 1)
    up_one.start(back_sent)
    back_far = after(back_far, up_one.sent)
    back_share = unsort_rows(own[2] + back_near.astype(F32) + back_far.astype(F32))
    gate_grad = jnp.sum(jnp.where(place, gate_sorted[:, None], 0.0), axis=0)

    logits = jnp.dot(normed_two, router_weight, preferred_element_type=F32)
    router_probs = jax.nn.softmax(logits, axis=-1)
    gate_prob = jnp.sum(router_probs * my_hot, axis=-1)
    grad_out = cotangent.astype(F32)
    logit_grad = ((gate_grad * gate_prob)[:, None] * (my_hot - router_probs)).astype(BF16)
    router_grad = jnp.einsum("td,te->de", normed_two, logit_grad, preferred_element_type=F32)
    normed_grad = back_share + jnp.einsum(
        "te,de->td", logit_grad, router_weight, preferred_element_type=F32
    )
    hidden_part, ffn_gain_grad = jax.vjp(norm_rows, hidden_share, ffn_gain)[1](normed_grad)
    hidden_grad = grad_out + hidden_part

    attn_grad = hidden_grad.astype(BF16)
    far_grad = swap(attn_grad, "tensor", 2)
    near_grad = swap(attn_grad, "tensor", 1)
    down_one.start(attn_grad)
    down_two.start(attn_grad)

    def in_order(mine, partner):
        return jnp.concatenate(
            [jnp.where(core == 0, mine, partner), jnp.where(core == 0, partner, mine)]
        )

    def mixed_grad(rows_grad):
        return jnp.einsum("df,td->ft", proj_weight, rows_grad, preferred_element_type=F32).astype(
            BF16
        )

    own_attn_grad = in_order(attn_grad, near_grad)
    own_mixed_grad = after(mixed_grad(own_attn_grad), down_one.sent, down_two.sent)
    own_qkv_grad, own_diag = backward_attention(
        own_seq, qkv, own_mixed_grad, lse_own, offsets, seq_len
    )
    far_grad = after(far_grad, own_qkv_grad)
    other_attn_grad = in_order(far_grad, swap(far_grad, "tensor", 1))
    held = after((own[0], own[1], other[0], other[1]), own_qkv_grad)
    out_passed = swap(held[3].astype(BF16), "tensor", 1)
    out_sent = (held[2] + out_passed.astype(F32)).astype(BF16)
    out_far = swap(out_sent, "tensor", 2)
    out_near = swap(held[1], "tensor", 1)
    up_one.start(own_qkv_grad)
    down_one.start(own_qkv_grad)
    up_two.start(own_qkv_grad)
    other_mixed_grad = after(
        mixed_grad(other_attn_grad), out_sent, up_one.sent, down_one.sent, up_two.sent
    )
    other_qkv_grad, other_diag = backward_attention(
        other_seq, qkv, other_mixed_grad, lse_other, offsets, seq_len
    )

    def input_part(qkv_rows, core_index):
        return jnp.einsum(
            "cft,cdf->td", columns(qkv_rows, core_index), qkv_weight, preferred_element_type=F32
        )

    input_passed = swap(input_part(other_qkv_grad, 1 - core).astype(BF16), "tensor", 1)
    input_sent = (input_part(other_qkv_grad, core) + input_passed.astype(F32)).astype(BF16)
    input_far = swap(input_sent, "tensor", 2)
    own_late = after(own_qkv_grad, input_sent)
    input_near = swap(input_part(own_late, 1 - core).astype(BF16), "tensor", 1)
    down_two.start(input_sent)
    up_one.start(input_sent)
    own_normed = lax.dynamic_slice_in_dim(normed_one, chip * half, half, 0)
    other_normed = lax.dynamic_slice_in_dim(normed_one, (1 - chip) * half, half, 0)
    qkv_grad = jnp.einsum(
        "td,cft->cdf", own_normed, own_late, preferred_element_type=F32
    ) + jnp.einsum("td,cft->cdf", other_normed, other_qkv_grad, preferred_element_type=F32)
    proj_grad = jnp.einsum(
        "td,ft->df", own_attn_grad, mixed_own, preferred_element_type=F32
    ) + jnp.einsum("td,ft->df", other_attn_grad, mixed_other, preferred_element_type=F32)
    projections = ScatterSum(jnp.concatenate([qkv_grad, proj_grad[None]]))
    projections.start(down_two.sent, up_one.sent)
    input_share_grad = (
        input_part(own_late, core)
        + input_near.astype(F32)
        + after(input_far, projections.sent).astype(F32)
    )
    token_part = jax.vjp(lambda rows_in: norm_rows(rows_in, attn_gain), input_share)[1](
        input_share_grad
    )[0]
    tokens_grad = hidden_grad + token_part
    attn_gain_grad = jnp.sum(qkv_weight.astype(F32) * qkv_grad, axis=(0, 2)) / attn_gain

    out_far = after(out_far, input_sent)
    expert_share = unsort_rows(held[0] + out_near.astype(F32) + out_far.astype(F32))
    layer_out = (hidden_share + gate_prob[:, None] * expert_share).astype(BF16)

    table_local = jnp.dot((own_diag + other_diag)[:, 0], bucket_hot, precision=highest)
    table_full = lax.dynamic_update_slice_in_dim(
        jnp.zeros((heads * tensor_count, bucket_count), F32), table_local, rank * heads, 0
    )
    small = [attn_gain_grad, ffn_gain_grad, router_grad.reshape(-1), table_full.reshape(-1)]
    sizes = [array.size for array in small]
    packed = jnp.concatenate(small)
    packed = jnp.pad(packed, (0, -packed.size % 1024)).reshape(-1, 128)
    packed = sum_everywhere(after(packed, projections.sent)).reshape(-1)
    ends = [sum(sizes[:i]) for i in range(5)]
    attn_gain_grad, ffn_gain_grad, router_grad, table_grad = [
        packed[ends[i] : ends[i + 1]] for i in range(4)
    ]
    up_two.start(input_share_grad)
    projections.start(input_share_grad)
    down_grad = jnp.concatenate([down_one.finish(), down_two.finish()])
    up_grad = jnp.concatenate([up_one.finish(), up_two.finish()])
    qkv_proj = projections.finish()
    return (
        layer_out,
        tokens_grad,
        attn_gain_grad,
        qkv_proj[:3],
        qkv_proj[3],
        table_grad.reshape(heads * tensor_count, bucket_count),
        ffn_gain_grad,
        router_grad.reshape(router_weight.shape),
        up_grad,
        down_grad,
    )


def solution(mesh):
    placed = (
        P("dp", None),
        P(),
        P(None, None, "tensor"),
        P(None, "tensor"),
        P("tensor", None),
        P(),
        P(),
        P(),
        P("dp", None),
        P(None, None, "tensor"),
        P(None, None, "tensor"),
        P(("dp", "tensor"), None),
    )
    return jax.shard_map(
        on_device,
        mesh=mesh,
        in_specs=placed,
        out_specs=(
            P(("dp", "tensor"), None),
            P(("dp", "tensor"), None),
            P(),
            P(None, "dp", "tensor"),
            P("dp", "tensor"),
            P(),
            P(),
            P(),
            P(None, "dp", "tensor"),
            P(None, "dp", "tensor"),
        ),
        check_vma=False,
    )
```

```python
import functools
import jax, jax.numpy as jnp
from jax import lax
from jax.experimental import pallas as pl
from jax.experimental.pallas import tpu as pltpu
from jax.sharding import PartitionSpec as P

QB = 256
KB = 128


def mm(a, b, dims):
    return lax.dot_general(a, b, (dims, ((), ())), preferred_element_type=jnp.float32)


def score_block(keys, queries, skew, first_query, seq_len):
    scores = mm(keys, queries, ((1,), (0,)))
    bias = [
        skew[:, pl.ds(pl.multiple_of(first_query - first_key + seq_len - KB, KB), QB)]
        for first_key in range(0, seq_len, KB)
    ]
    return scores + jnp.concatenate(bias, axis=0)


def forward_kernel(seq_ref, qkv_ref, offset_ref, mixed_ref, lse_ref, skew):
    seq_len = qkv_ref.shape[2]
    scale = qkv_ref.shape[1] ** -0.5
    skew[...] = pltpu.roll(
        jnp.broadcast_to(offset_ref[0], (KB, 2 * seq_len)), 0, 1, stride=1, stride_axis=0
    )
    keys = qkv_ref[1].T
    values = qkv_ref[2]

    def block(index, carry):
        first = pl.multiple_of(index * QB, QB)
        queries = qkv_ref[0, :, pl.ds(first, QB)] * jnp.bfloat16(scale)
        scores = score_block(keys, queries, skew, first, seq_len)
        largest = jnp.max(scores, axis=0, keepdims=True)
        expos = jnp.exp(scores - largest)
        total = jnp.sum(expos, axis=0, keepdims=True)
        weights = (expos * (1.0 / total)).astype(jnp.bfloat16)
        mixed_ref[:, pl.ds(first, QB)] = mm(values, weights, ((1,), (0,))).astype(jnp.bfloat16)
        lse_ref[0, :, pl.ds(first, QB)] = largest + jnp.log(total)
        return carry

    lax.fori_loop(0, seq_len // QB, block, 0, unroll=True)


def forward_attention(seq, qkv, offsets, seq_len):
    _, width, rows = qkv.shape
    heads = offsets.shape[0]
    size = width // heads
    return pl.pallas_call(
        forward_kernel,
        grid_spec=pltpu.PrefetchScalarGridSpec(
            num_scalar_prefetch=1,
            grid=(heads,),
            in_specs=[
                pl.BlockSpec((3, size, seq_len), lambda h, s: (0, h, s[0])),
                pl.BlockSpec((1, 1, 2 * seq_len), lambda h, s: (h, 0, 0)),
            ],
            out_specs=[
                pl.BlockSpec((size, seq_len), lambda h, s: (h, 0)),
                pl.BlockSpec((1, 1, seq_len), lambda h, s: (h, 0, 0)),
            ],
            scratch_shapes=[pltpu.VMEM((KB, 2 * seq_len), jnp.float32)],
        ),
        out_shape=[
            jax.ShapeDtypeStruct((width, seq_len), jnp.bfloat16),
            jax.ShapeDtypeStruct((heads, 1, seq_len), jnp.float32),
        ],
        compiler_params=pltpu.CompilerParams(vmem_limit_bytes=48 * 2**20),
        cost_estimate=pl.CostEstimate(flops=1, bytes_accessed=1, transcendentals=0),
        name="attention_forward",
    )(seq, qkv, offsets)


def backward_kernel(
    seq_ref, qkv_ref, grad_ref, lse_ref, offset_ref, out_ref, diag_ref, skew, sums, probs_all, score_all
):
    seq_len = qkv_ref.shape[2]
    scale = qkv_ref.shape[1] ** -0.5
    skew[...] = pltpu.roll(
        jnp.broadcast_to(offset_ref[0], (KB, 2 * seq_len)), 0, 1, stride=1, stride_axis=0
    )
    sums[...] = jnp.zeros_like(sums)
    keys_t = qkv_ref[1]
    keys = keys_t.T
    values = qkv_ref[2].T

    def block(index, carry):
        first = pl.multiple_of(index * QB, QB)
        here = pl.ds(first, QB)
        queries = qkv_ref[0, :, here] * jnp.bfloat16(scale)
        scores = score_block(keys, queries, skew, first, seq_len)
        probs = jnp.exp(scores - lse_ref[0, :, here])
        probs_all[:, here] = probs.astype(jnp.bfloat16)
        prob_grad = mm(values, grad_ref[:, here], ((1,), (0,)))
        centre = jnp.sum(probs * prob_grad, axis=0, keepdims=True)
        score_grad = probs * (prob_grad - centre)
        rounded = score_grad.astype(jnp.bfloat16)
        score_all[:, here] = rounded
        for first_key in range(0, seq_len, KB):
            spot = pl.ds(pl.multiple_of(first - first_key + seq_len - KB, KB), QB)
            sums[:, spot] += score_grad[first_key : first_key + KB]
        out_ref[0, :, here] = (mm(keys_t, rounded, ((1,), (0,))) * scale).astype(jnp.bfloat16)
        return carry

    lax.fori_loop(0, seq_len // QB, block, 0, unroll=True)
    queries = qkv_ref[0] * jnp.bfloat16(scale)
    out_ref[1] = mm(queries, score_all[...], ((1,), (1,))).astype(jnp.bfloat16)
    out_ref[2] = mm(grad_ref[...], probs_all[...], ((1,), (1,))).astype(jnp.bfloat16)
    part = sums[...]
    half = KB // 2
    while half >= 1:
        part = part[:half] + pltpu.roll(part[half:], 2 * seq_len - half, 1)
        half //= 2
    diag_ref[0] = part


def backward_attention(seq, qkv, grads, lse, offsets, seq_len):
    _, width, rows = qkv.shape
    heads = offsets.shape[0]
    size = width // heads
    return pl.pallas_call(
        backward_kernel,
        grid_spec=pltpu.PrefetchScalarGridSpec(
            num_scalar_prefetch=1,
            grid=(heads,),
            in_specs=[
                pl.BlockSpec((3, size, seq_len), lambda h, s: (0, h, s[0])),
                pl.BlockSpec((size, seq_len), lambda h, s: (h, 0)),
                pl.BlockSpec((1, 1, seq_len), lambda h, s: (h, 0, 0)),
                pl.BlockSpec((1, 1, 2 * seq_len), lambda h, s: (h, 0, 0)),
            ],
            out_specs=[
                pl.BlockSpec((3, size, seq_len), lambda h, s: (0, h, 0)),
                pl.BlockSpec((1, 1, 2 * seq_len), lambda h, s: (h, 0, 0)),
            ],
            scratch_shapes=[
                pltpu.VMEM((KB, 2 * seq_len), jnp.float32),
                pltpu.VMEM((KB, 2 * seq_len), jnp.float32),
                pltpu.VMEM((seq_len, seq_len), jnp.bfloat16),
                pltpu.VMEM((seq_len, seq_len), jnp.bfloat16),
            ],
        ),
        out_shape=[
            jax.ShapeDtypeStruct((3, width, seq_len), jnp.bfloat16),
            jax.ShapeDtypeStruct((heads, 1, 2 * seq_len), jnp.float32),
        ],
        compiler_params=pltpu.CompilerParams(vmem_limit_bytes=48 * 2**20),
        cost_estimate=pl.CostEstimate(flops=1, bytes_accessed=1, transcendentals=0),
        name="attention_backward",
    )(seq, qkv, grads, lse, offsets)


CH = 16
UNIT = 128
FIELDS = 4


def unit_limit(rows, shares, experts):
    chunks = rows // CH + shares * (experts - 1)
    return (chunks + experts * (UNIT // CH - 1)) // (UNIT // CH)


def plan_segments(counts):
    starts = jnp.cumsum(counts, axis=1) - counts
    first = starts // CH
    chunks = jnp.where(counts > 0, (starts + counts + CH - 1) // CH - first, 0)
    units = (jnp.sum(chunks, axis=0) * CH + UNIT - 1) // UNIT
    base = jnp.cumsum(units) - units
    return jnp.concatenate(
        [first, chunks, starts, starts + counts, units[None], base[None]], axis=0
    ).astype(jnp.int32)


def for_units(units, step):
    def double(index, carry):
        step(index * (2 * UNIT), 2 * UNIT)
        return carry

    lax.fori_loop(0, units // 2, double, 0)

    @pl.when(units % 2 == 1)
    def _():
        step((units - 1) * UNIT, UNIT)


def at_rows(start, size):
    return pl.ds(pl.multiple_of(start, size if size < UNIT else UNIT), size)


def gather_rows(plan_ref, expert, shares, units, rows_refs, grad_refs, xs, cs, base):
    filled = 0
    for share in range(shares):
        first = plan_ref[share, expert]
        chunks = plan_ref[shares + share, expert]
        start = plan_ref[2 * shares + share, expert]
        end = plan_ref[3 * shares + share, expert]
        x_ref, c_ref = rows_refs[share], grad_refs[share]

        def gather(index, carry):
            here = (first + index) * CH
            local = (filled + index) * CH
            row = here + lax.broadcasted_iota(jnp.int32, (CH, 1), 0)
            keep = (row >= start) & (row < end)
            zero = jnp.zeros((), jnp.bfloat16)
            xs[at_rows(base + local, CH)] = jnp.where(keep, x_ref[at_rows(here, CH)], zero)
            cs[at_rows(local, CH)] = jnp.where(keep, c_ref[at_rows(here, CH)], zero)
            return carry

        lax.fori_loop(0, chunks, gather, 0)
        filled = filled + chunks

    def clear(index, carry):
        xs[at_rows(base + index * CH, CH)] = jnp.zeros((CH, xs.shape[1]), jnp.bfloat16)
        cs[at_rows(index * CH, CH)] = jnp.zeros((CH, cs.shape[1]), jnp.bfloat16)
        return carry

    lax.fori_loop(filled, units * (UNIT // CH), clear, 0)


def scatter_rows(plan_ref, expert, shares, buffers, outs):
    filled = 0
    for share in range(shares):
        first = plan_ref[share, expert]
        chunks = plan_ref[shares + share, expert]

        def scatter(index, carry):
            target = at_rows((first + index) * CH, CH)
            local = at_rows((filled + index) * CH, CH)
            for buffer, targets in zip(buffers, outs):
                out = targets[share]
                out[target] = (out[target].astype(jnp.float32) + buffer[local]).astype(out.dtype)
            return carry

        lax.fori_loop(0, chunks, scatter, 0)
        filled = filled + chunks


def store_parts(outs, values, side, bit, piece):
    if len(outs) == 1:
        outs[0][0] = values[...].astype(jnp.bfloat16)
        return
    for index in range(values.shape[0] // (2 * piece)):
        low, high = index % bit, index // bit
        for which, out in enumerate(outs):
            chosen = side if which == 0 else 1 - side
            start = ((high * 2 + chosen) * bit + low) * piece
            rows = values[pl.ds(pl.multiple_of(start, CH), piece)]
            out[0, index] = rows.astype(jnp.bfloat16)


def expert_kernel(*refs, shares, first_expert, expert_count, with_grads, bits, piece):
    plan_ref, refs = refs[0], refs[1:]
    if with_grads:
        past_plan, side_ref, refs = refs[0], refs[1], refs[2:]
    x_refs, refs = refs[:shares], refs[shares:]
    c_refs, refs = refs[:shares], refs[shares:]
    router_ref, up_ref, down_ref, *refs = refs
    if with_grads:
        past, refs = refs[:4], refs[4:]
    y_refs, refs = refs[:shares], refs[shares:]
    back_refs, refs = refs[:shares], refs[shares:]
    gate_refs, refs = refs[:shares], refs[shares:]
    if with_grads:
        parts = 2 if bits else 1
        up_outs, refs = refs[:parts], refs[parts:]
        down_outs, refs = refs[:parts], refs[parts:]
        xs, ms, dys, dus, *refs = refs
        cs, ybuf, bbuf, gbuf, *refs = refs
        gates, refs = refs[:shares], refs[shares:]
        old, up_acc, down_acc, sems = refs[:4], refs[4], refs[5], refs[6]
    else:
        xs, ms, dys, dus, cs, ybuf, bbuf, gbuf, *gates = refs
    step = pl.program_id(0)
    expert = step + first_expert
    units = plan_ref[4 * shares, expert]
    base = 0 if with_grads else plan_ref[4 * shares + 1, expert] * UNIT

    @pl.when(step == 0)
    def _():
        for out in (*y_refs, *back_refs, *gates):
            out[...] = jnp.zeros_like(out)

    if with_grads:
        past_units = past_plan[4 * shares, expert]
        past_base = past_plan[4 * shares + 1, expert] * UNIT

        def copies(index):
            return [
                pltpu.make_async_copy(
                    source.at[at_rows(past_base + index * UNIT, UNIT)],
                    target.at[at_rows(index * UNIT, UNIT)],
                    sems.at[which, index],
                )
                for which, (source, target) in enumerate(zip(past, old))
            ]

        def begin(index, carry):
            for copy in copies(index):
                copy.start()
            return carry

        def finish(index, carry):
            for copy in copies(index):
                copy.wait()
            return carry

        lax.fori_loop(0, past_units, begin, 0)

    gather_rows(plan_ref, expert, shares, units, x_refs, c_refs, xs, cs, base)

    def tile(start, size):
        local = at_rows(start, size)
        saved = at_rows(base + start, size)
        x = xs[saved]
        c = cs[local].astype(jnp.float32)
        logits = mm(x, router_ref[...], ((1,), (0,)))
        lane = lax.broadcasted_iota(jnp.int32, logits.shape, 1)
        logits = jnp.where(lane < expert_count, logits, -jnp.inf)
        expos = jnp.exp(logits - jnp.max(logits, axis=1, keepdims=True))
        mine = jnp.sum(jnp.where(lane == expert, expos, 0.0), axis=1, keepdims=True)
        gate = mine / jnp.sum(expos, axis=1, keepdims=True)
        dy = (gate * c).astype(jnp.bfloat16)
        dys[saved] = dy
        u = mm(x, up_ref[0], ((1,), (0,)))
        dm = mm(dy, down_ref[0], ((1,), (0,)))
        root = 0.7978845608028654
        square = u * u
        bent = jnp.tanh(root * (u * (1.0 + 0.044715 * square)))
        half = 0.5 * (1.0 + bent)
        m = (u * half).astype(jnp.bfloat16)
        ms[saved] = m
        slope = half + (0.5 * root) * (u * ((1.0 - bent * bent) * (1.0 + (3 * 0.044715) * square)))
        du = (slope * dm).astype(jnp.bfloat16)
        dus[saved] = du
        y = mm(m, down_ref[0], ((1,), (1,)))
        ybuf[local] = y
        gbuf[local] = jnp.broadcast_to(jnp.sum(y * c, axis=1, keepdims=True), (size, gbuf.shape[1]))
        bbuf[local] = mm(du, up_ref[0], ((1,), (1,)))

    for_units(units, tile)
    scatter_rows(
        plan_ref, expert, shares, (ybuf, bbuf, gbuf), (y_refs, back_refs, gates)
    )

    @pl.when(step == pl.num_programs(0) - 1)
    def _():
        for gate, out in zip(gates, gate_refs):
            out[...] = gate[...].T[:1]

    if with_grads:
        up_acc[...] = jnp.zeros_like(up_acc)
        down_acc[...] = jnp.zeros_like(down_acc)

        def add(arrays):
            def part(start, size):
                here = at_rows(start, size)
                x, m, dy, du = [array[here] for array in arrays]
                up_acc[...] += mm(x, du, ((0,), (0,)))
                down_acc[...] += mm(dy, m, ((0,), (0,)))

            return part

        for_units(units, add((xs, ms, dys, dus)))
        lax.fori_loop(0, past_units, finish, 0)
        for_units(past_units, add(old))
        up_bit, down_bit = bits or (0, 0)
        store_parts(up_outs, up_acc, side_ref[0], up_bit, piece)
        store_parts(down_outs, down_acc, side_ref[1], down_bit, piece)


def run_experts(plan, x, c, router, up, down, past=None, first_expert=0, step_count=None):
    shares = len(x)
    rows, width = x[0].shape
    experts, _, hidden = up.shape
    steps = step_count or experts
    with_grads = past is not None
    saved = unit_limit(rows * shares, shares, experts) * UNIT
    most = rows * shares
    brain, full = jnp.bfloat16, jnp.float32
    whole = lambda shape: pl.BlockSpec(shape, lambda e, *p: (0, 0))
    block = pl.BlockSpec((1, width, hidden), lambda e, *p: (first_expert + e, 0, 0))
    scalars = [plan]
    inputs = [*x, *c, router, up, down]
    in_specs = [whole((rows, width))] * (2 * shares) + [whole(router.shape), block, block]
    row_types = [full] + [brain] * (shares - 1)
    out_shape = [jax.ShapeDtypeStruct((rows, width), kind) for kind in row_types * 2]
    out_specs = [whole((rows, width))] * (2 * shares) + [whole((1, rows))] * shares
    out_shape += [jax.ShapeDtypeStruct((1, rows), full)] * shares
    scratch = [
        pltpu.VMEM((most, width), brain),
        pltpu.VMEM((most, width), full),
        pltpu.VMEM((most, width), full),
        pltpu.VMEM((most, 128), full),
    ] + [pltpu.VMEM((rows, 128), full)] * shares
    widths = (width, hidden, width, hidden)
    if with_grads:
        past_plan, past_arrays, sides, bits, piece = past
        scalars += [past_plan, sides]
        inputs += past_arrays
        in_specs += [pl.BlockSpec(memory_space=pl.ANY)] * 4
        if bits:
            shape = (width // (2 * piece), piece, hidden)
            out_specs += [pl.BlockSpec((1, *shape), lambda e, *p: (e, 0, 0, 0))] * 4
            out_shape += [jax.ShapeDtypeStruct((steps, *shape), brain)] * 4
        else:
            out_specs += [pl.BlockSpec((1, width, hidden), lambda e, *p: (e, 0, 0))] * 2
            out_shape += [jax.ShapeDtypeStruct((steps, width, hidden), brain)] * 2
        buffers = [pltpu.VMEM((most, size), brain) for size in widths]
        scratch = (
            buffers
            + scratch
            + buffers
            + [pltpu.VMEM((width, hidden), full)] * 2
            + [pltpu.SemaphoreType.DMA((4, most // UNIT))]
        )
    else:
        out_specs += [whole((saved, size)) for size in widths]
        out_shape += [jax.ShapeDtypeStruct((saved, size), brain) for size in widths]
    return pl.pallas_call(
        functools.partial(
            expert_kernel,
            shares=shares,
            first_expert=first_expert,
            expert_count=experts,
            with_grads=with_grads,
            bits=bits if with_grads else None,
            piece=piece if with_grads else None,
        ),
        grid_spec=pltpu.PrefetchScalarGridSpec(
            num_scalar_prefetch=len(scalars),
            grid=(steps,),
            in_specs=in_specs,
            out_specs=out_specs,
            scratch_shapes=scratch,
        ),
        out_shape=out_shape,
        compiler_params=pltpu.CompilerParams(vmem_limit_bytes=58 * 2**20),
        cost_estimate=pl.CostEstimate(flops=1, bytes_accessed=1, transcendentals=0),
        name="experts_and_grads" if with_grads else "experts",
    )(*scalars, *inputs)


def input_kernel(core_ref, grad_ref, weight_ref, keep_ref, send_ref):
    share = keep_ref.shape[0]
    for target, out in ((core_ref[0], keep_ref), (1 - core_ref[0], send_ref)):
        here = pl.ds(pl.multiple_of(target * share, share), share)
        total = sum(
            mm(grad_ref[which, :, here].T, weight_ref[which], ((1,), (1,))) for which in range(3)
        )
        out[...] = total.astype(out.dtype)


def input_grads(core, qkv_rows, qkv_weight):
    share = qkv_rows.shape[2] // 2
    width = qkv_weight.shape[1]
    vmem = pl.BlockSpec(memory_space=pltpu.VMEM)
    return pl.pallas_call(
        input_kernel,
        in_specs=[pl.BlockSpec(memory_space=pltpu.SMEM), vmem, vmem],
        out_specs=[vmem, vmem],
        out_shape=[
            jax.ShapeDtypeStruct((share, width), jnp.float32),
            jax.ShapeDtypeStruct((share, width), jnp.bfloat16),
        ],
        compiler_params=pltpu.CompilerParams(vmem_limit_bytes=40 * 2**20),
        name="input_grads",
    )(core, qkv_rows, qkv_weight)


def projection_kernel(*refs):
    _, _, *refs = refs
    (rows_a, rows_b, grad_a, grad_b, out_a, out_b, mixed_a, mixed_b, weight, total, gain) = refs
    gain_total = jnp.zeros(gain.shape, jnp.float32)
    for which in range(3):
        part = mm(grad_a[which], rows_a[...], ((1,), (0,)))
        part = part + mm(grad_b[which], rows_b[...], ((1,), (0,)))
        total[which] = part.T.astype(jnp.bfloat16)
        turned = weight[which].astype(jnp.float32).T
        gain_total = gain_total + jnp.sum(turned * part, axis=0, keepdims=True)
    part = mm(mixed_a[...], out_a[...], ((1,), (0,))) + mm(mixed_b[...], out_b[...], ((1,), (0,)))
    total[3] = part.T.astype(jnp.bfloat16)
    gain[...] = gain_total


def projection_grads(seqs, normed, qkv_rows, out_rows, mixed, qkv_weight):
    _, size, seq_len = qkv_rows[0].shape
    width = normed.shape[1]
    whole = lambda array: pl.BlockSpec(array.shape, lambda i, a, b: (0,) * array.ndim)
    operands = [normed, normed, *qkv_rows, *out_rows, *mixed, qkv_weight]
    in_specs = [
        pl.BlockSpec((seq_len, width), lambda i, a, b: (a[0], 0)),
        pl.BlockSpec((seq_len, width), lambda i, a, b: (b[0], 0)),
    ] + [whole(array) for array in operands[2:]]
    return pl.pallas_call(
        projection_kernel,
        grid_spec=pltpu.PrefetchScalarGridSpec(
            num_scalar_prefetch=2,
            grid=(1,),
            in_specs=in_specs,
            out_specs=[
                pl.BlockSpec((4, width, size), lambda i, a, b: (0, 0, 0)),
                pl.BlockSpec((1, width), lambda i, a, b: (0, 0)),
            ],
        ),
        out_shape=[
            jax.ShapeDtypeStruct((4, width, size), jnp.bfloat16),
            jax.ShapeDtypeStruct((1, width), jnp.float32),
        ],
        compiler_params=pltpu.CompilerParams(vmem_limit_bytes=56 * 2**20),
        name="projection_grads",
    )(*seqs, *operands)


EPS = 1e-06
F32 = jnp.float32
BF16 = jnp.bfloat16


def norm_rows(values, gain_vector):
    return values * lax.rsqrt(jnp.mean(values * values, axis=-1, keepdims=True) + EPS) * gain_vector


def swap(values, axis, bit):
    count = lax.axis_size(axis)
    return lax.ppermute(values, axis, [(i, i ^ bit) for i in range(count)])


def after(value, *milestones):
    return lax.optimization_barrier((value, milestones))[0]


def join(values, *moving):
    values, landed = lax.optimization_barrier((values, tuple(move.moving for move in moving)))
    for move, received in zip(moving, landed):
        move.moving = received
    return values


class Transfer:
    def __init__(self, values, axis, bit):
        self.moving = swap(values, axis, bit)


class ScatterSum:
    def __init__(self, parts, bits):
        self.bits = list(bits)
        self.left = sorted(bits, reverse=True)
        self.moving = None
        self.parts = None
        experts, width = parts[0].shape[0], parts[0].shape[-1]
        sizes = [2] * len(self.bits)
        if len(parts) == 1:
            values = parts[0]
            self.values = values.reshape(experts, *sizes, values.shape[1] >> len(sizes), width)
        else:
            self.parts = parts
            self.shape = (experts, *sizes[1:], parts[0].shape[-2], width)

    def pick(self, other):
        mine = (lax.axis_index("dp") // self.bit) % 2
        index = 1 - mine if other else mine
        return lax.dynamic_index_in_dim(self.values, index, self.spot, keepdims=False)

    def land(self):
        keep = self.parts[0] if self.parts else self.pick(False)
        self.values = keep.astype(F32) + self.moving.astype(F32)
        if self.parts:
            self.values = self.values.reshape(self.shape)
        self.parts = None
        self.moving = None
        self.left.remove(self.bit)

    def launch(self, *milestones):
        if self.moving is not None:
            self.land()
        if not self.bits:
            return
        self.bit = self.bits.pop(0)
        self.spot = 1 + self.left.index(self.bit)
        if self.parts:
            self.sent = after(self.parts[1], *milestones) if milestones else self.parts[1]
        else:
            self.values = after(self.values, *milestones) if milestones else self.values
            self.sent = self.pick(True).astype(BF16)
        self.moving = swap(self.sent, "dp", self.bit)

    def finish(self):
        while self.moving is not None:
            self.launch()
        return self.values


def sum_everywhere(values):
    for axis in ("tensor", "dp"):
        bit = 1
        while bit < lax.axis_size(axis):
            values = values + swap(values, axis, bit)
            bit *= 2
    return values


def on_device(
    tokens,
    attn_gain,
    qkv_weight,
    proj_weight,
    bias_table,
    buckets,
    ffn_gain,
    router_weight,
    routes,
    up_weight,
    down_weight,
    cotangent,
):
    highest = lax.Precision.HIGHEST
    rank = lax.axis_index("tensor")
    core, chip = rank % 2, rank // 2
    tensor_count = lax.axis_size("tensor")
    rows, width = tokens.shape
    share = rows // tensor_count
    half = rows // 2
    seq_len = (buckets.shape[0] + 1) // 2
    heads, bucket_count = bias_table.shape
    experts = up_weight.shape[0]
    own_seq = chip.astype(jnp.int32).reshape(1)
    other_seq = 1 - own_seq

    flipped = buckets[::-1]
    cut = KB - 1
    turned = jnp.concatenate([flipped[cut:], jnp.full((1,), -1, flipped.dtype), flipped[:cut]])
    bucket_hot = (turned[:, None] == jnp.arange(bucket_count)[None, :]).astype(F32)
    offsets = jnp.dot(bias_table, bucket_hot.T, precision=highest)[:, None, :]

    all_routes = routes[:, 0].reshape(tensor_count, share)
    counts = jnp.sum((all_routes[:, :, None] == jnp.arange(experts)).astype(jnp.int32), axis=1)
    order = rank ^ jnp.arange(tensor_count)
    same = order[:, None] == jnp.arange(tensor_count)[None, :]
    counts = jnp.sum(jnp.where(same[:, :, None], counts[None], 0), axis=1)
    own_plan = plan_segments(counts[:2])
    other_plan = plan_segments(counts[2:])
    my_routes = lax.dynamic_slice_in_dim(routes[:, 0], rank * share, share, 0)
    my_hot = (my_routes[:, None] == jnp.arange(experts)[None, :]).astype(F32)
    earlier = (jnp.arange(share)[:, None] > jnp.arange(share)[None, :]).astype(BF16)
    ahead = jnp.dot(earlier, my_hot.astype(BF16), preferred_element_type=F32)
    starts = (jnp.cumsum(counts[0]) - counts[0]).astype(F32)
    position = jnp.sum(my_hot * (ahead + starts[None, :]), axis=1).astype(jnp.int32)
    place = jnp.arange(share)[:, None] == position[None, :]
    place_matrix = place.astype(BF16)

    def sort_rows(values):
        return jnp.dot(place_matrix, values, preferred_element_type=F32).astype(BF16)

    def unsort_rows(values):
        dims = (((0,), (0,)), ((), ()))
        high = lax.reduce_precision(values, 8, 7)
        low = (values - high).astype(BF16)
        return lax.dot_general(
            place_matrix, high.astype(BF16), dims, preferred_element_type=F32
        ) + lax.dot_general(place_matrix, low, dims, preferred_element_type=F32)

    grad_mine = sort_rows(cotangent)
    grad_near = swap(grad_mine, "tensor", 1)
    grad_far = Transfer(grad_mine, "tensor", 2)
    padded_router = jnp.pad(router_weight, ((0, 0), (0, 128 - experts)))
    early = (grad_mine, grad_near, place_matrix, own_plan, other_plan, padded_router, my_hot)

    normed_one = norm_rows(after(tokens, *early).astype(F32), attn_gain).astype(BF16)
    input_share = lax.dynamic_slice_in_dim(tokens, rank * share, share, 0).astype(F32)
    qkv = jnp.einsum("cdf,td->cft", qkv_weight, normed_one, preferred_element_type=F32).astype(BF16)

    def columns(values, core_index):
        return lax.dynamic_slice_in_dim(values, core_index * share, share, values.ndim - 1)

    def project(mixed, core_index):
        return jnp.einsum(
            "ft,df->td", columns(mixed, core_index), proj_weight, preferred_element_type=F32
        )

    mixed_other, lse_other = join(
        forward_attention(other_seq, qkv, offsets, seq_len), grad_far
    )
    passed = swap(project(mixed_other, 1 - core).astype(BF16), "tensor", 1)
    attn_sent = (project(mixed_other, core) + passed.astype(F32)).astype(BF16)
    attn_far = Transfer(attn_sent, "tensor", 2)
    grad_far = grad_far.moving
    grad_both = swap(grad_far, "tensor", 1)
    mixed_own, lse_own = join(
        forward_attention(after(own_seq, attn_sent, grad_both), qkv, offsets, seq_len), attn_far
    )
    attn_near = swap(project(mixed_own, 1 - core).astype(BF16), "tensor", 1)
    attn_share = project(mixed_own, core) + attn_near.astype(F32) + attn_far.moving.astype(F32)
    hidden_share = input_share + attn_share
    normed_two = norm_rows(hidden_share, ffn_gain).astype(BF16)

    rows_mine = sort_rows(normed_two)
    rows_far = Transfer(rows_mine, "tensor", 2)
    rows_near = swap(rows_mine, "tensor", 1)
    own = run_experts(
        own_plan, [rows_mine, rows_near], [grad_mine, grad_near], padded_router, up_weight, down_weight
    )
    own = join(own, rows_far)
    count = lax.axis_size("dp")
    index = lax.axis_index("dp")
    bits = [1 << i for i in range(count.bit_length() - 1)]
    turned_bits = bits[1:] + bits[:1]
    piece = width // count
    aligned = piece % CH == 0
    back_near = swap(own[3], "tensor", 1)
    gate_near = swap(own[5][0], "tensor", 1)
    rows_far = rows_far.moving
    other_rows = [rows_far, swap(rows_far, "tensor", 1)]
    split = experts // 2

    def run_other(plan, start, firsts):
        sides = jnp.stack([index // bit % 2 for bit in firsts]).astype(jnp.int32)
        past = (own_plan, own[6:], sides, firsts if aligned else None, piece)
        return run_experts(
            plan, other_rows, [grad_far, grad_both], padded_router, up_weight, down_weight,
            past, start, split,
        )

    parts = 2 if aligned else 1
    first = run_other(
        after(other_plan, back_near, gate_near), 0, (turned_bits[0], bits[0])
    )
    down_one = ScatterSum(first[6 + parts :], bits)
    up_one = ScatterSum(first[6 : 6 + parts], turned_bits)
    down_one.launch()
    up_one.launch()
    second = join(
        run_other(after(other_plan, down_one.sent, up_one.sent), split, (bits[0], bits[0])),
        down_one,
        up_one,
    )
    other = [one.astype(F32) + two.astype(F32) for one, two in zip(first[:6], second[:6])]
    back_passed = swap(other[3].astype(BF16), "tensor", 1)
    gate_passed = swap(other[5][0], "tensor", 1)
    back_sent = (other[2] + back_passed.astype(F32)).astype(BF16)
    gate_far = Transfer(other[4][0] + gate_passed, "tensor", 2)
    back_far = Transfer(back_sent, "tensor", 2)
    down_two = ScatterSum(second[6 + parts :], bits)
    up_two = ScatterSum(second[6 : 6 + parts], bits)
    down_two.launch()
    down_one.moving, up_one.moving = after((down_one.moving, up_one.moving), back_sent)
    up_one.launch()
    down_one.launch()
    back_far = join(back_far.moving, down_two, down_one, up_one, gate_far)
    gate_sorted = own[4][0] + gate_near + gate_far.moving
    back_share = unsort_rows(own[2] + back_near.astype(F32) + back_far.astype(F32))
    gate_grad = jnp.sum(jnp.where(place, gate_sorted[:, None], 0.0), axis=0)

    logits = jnp.dot(normed_two, router_weight, preferred_element_type=F32)
    router_probs = jax.nn.softmax(logits, axis=-1)
    gate_prob = jnp.sum(router_probs * my_hot, axis=-1)
    grad_out = cotangent.astype(F32)
    logit_grad = ((gate_grad * gate_prob)[:, None] * (my_hot - router_probs)).astype(BF16)
    router_grad = jnp.einsum("td,te->de", normed_two, logit_grad, preferred_element_type=F32)
    normed_grad = back_share + jnp.einsum(
        "te,de->td", logit_grad, router_weight, preferred_element_type=F32
    )
    hidden_part, ffn_gain_grad = jax.vjp(norm_rows, hidden_share, ffn_gain)[1](normed_grad)
    hidden_grad = grad_out + hidden_part

    attn_grad = hidden_grad.astype(BF16)
    far_grad = Transfer(attn_grad, "tensor", 2)
    near_grad = swap(attn_grad, "tensor", 1)
    up_two.launch(attn_grad)
    down_two.moving, down_one.moving = after((down_two.moving, down_one.moving), attn_grad)
    down_two.launch()
    down_one.launch()

    def in_order(mine, partner):
        return jnp.concatenate(
            [jnp.where(core == 0, mine, partner), jnp.where(core == 0, partner, mine)]
        )

    def mixed_grad(rows_grad):
        return jnp.einsum("df,td->ft", proj_weight, rows_grad, preferred_element_type=F32).astype(
            BF16
        )

    own_attn_grad = in_order(attn_grad, near_grad)
    own_mixed_grad = after(mixed_grad(own_attn_grad), up_two.sent, down_one.sent, down_two.sent)
    own_qkv_grad, own_diag = join(
        backward_attention(own_seq, qkv, own_mixed_grad, lse_own, offsets, seq_len),
        far_grad,
        up_two,
        down_one,
        down_two,
    )
    far_grad = far_grad.moving
    other_attn_grad = in_order(far_grad, swap(far_grad, "tensor", 1))
    held = after((own[0], own[1], other[0], other[1]), own_qkv_grad)
    out_near = swap(held[1], "tensor", 1)
    out_passed = swap(held[3].astype(BF16), "tensor", 1)
    out_sent = (held[2] + out_passed.astype(F32)).astype(BF16)
    out_far = Transfer(out_sent, "tensor", 2)
    up_one.moving, down_two.moving = after((up_one.moving, down_two.moving), own_qkv_grad)
    up_one.launch()
    down_two.launch()
    up_two.launch()
    other_mixed_grad = after(
        mixed_grad(other_attn_grad), out_sent, out_near, up_one.sent, down_two.sent, up_two.sent
    )
    other_qkv_grad, other_diag = join(
        backward_attention(other_seq, qkv, other_mixed_grad, lse_other, offsets, seq_len),
        out_far,
        up_one,
        down_two,
        up_two,
    )
    out_far = out_far.moving

    core_index = core.astype(jnp.int32).reshape(1)
    up_two.launch()
    normed, own_late = after((normed_one, own_qkv_grad), up_two.sent)
    qkv_proj, gain_part = projection_grads(
        (own_seq, other_seq),
        normed,
        (own_late, other_qkv_grad),
        (own_attn_grad, other_attn_grad),
        (mixed_own, mixed_other),
        qkv_weight,
    )
    projections = ScatterSum([qkv_proj], bits)
    projections.launch()
    core_index = after(core_index, projections.sent)
    input_keep, input_send = input_grads(core_index, other_qkv_grad, qkv_weight)
    input_passed = swap(input_send, "tensor", 1)
    input_sent = (input_keep + input_passed.astype(F32)).astype(BF16)
    input_far = Transfer(input_sent, "tensor", 2)
    input_own, input_send = input_grads(after(core_index, input_sent), own_late, qkv_weight)
    input_near = swap(input_send, "tensor", 1)
    late = join(after(input_own, input_near), input_far, projections, up_two)
    input_share_grad = late + input_near.astype(F32) + input_far.moving.astype(F32)
    projections.launch()
    token_part = jax.vjp(lambda rows_in: norm_rows(rows_in, attn_gain), input_share)[1](
        input_share_grad
    )[0]
    tokens_grad = hidden_grad + token_part
    attn_gain_grad = gain_part[0] / attn_gain

    expert_share = unsort_rows(held[0] + out_near.astype(F32) + out_far.astype(F32))
    layer_out = (hidden_share + gate_prob[:, None] * expert_share).astype(BF16)

    table_local = jnp.dot((own_diag + other_diag)[:, 0], bucket_hot, precision=highest)
    table_full = lax.dynamic_update_slice_in_dim(
        jnp.zeros((heads * tensor_count, bucket_count), F32), table_local, rank * heads, 0
    )
    small = [attn_gain_grad, ffn_gain_grad, router_grad.reshape(-1), table_full.reshape(-1)]
    sizes = [array.size for array in small]
    packed = jnp.concatenate(small)
    packed = jnp.pad(packed, (0, -packed.size % 1024)).reshape(-1, 128)
    packed = sum_everywhere(after(packed, input_share_grad, projections.sent)).reshape(-1)
    ends = [sum(sizes[:i]) for i in range(5)]
    attn_gain_grad, ffn_gain_grad, router_grad, table_grad = [
        packed[ends[i] : ends[i + 1]] for i in range(4)
    ]
    down_grad = jnp.concatenate([down_one.finish(), down_two.finish()])
    up_grad = jnp.concatenate([up_one.finish(), up_two.finish()])
    qkv_proj = projections.finish()
    return (
        layer_out,
        tokens_grad,
        attn_gain_grad,
        qkv_proj[:3],
        qkv_proj[3],
        table_grad.reshape(heads * tensor_count, bucket_count),
        ffn_gain_grad,
        router_grad.reshape(router_weight.shape),
        up_grad,
        down_grad,
    )


def solution(mesh):
    placed = (
        P("dp", None),
        P(),
        P(None, None, "tensor"),
        P(None, "tensor"),
        P("tensor", None),
        P(),
        P(),
        P(),
        P("dp", None),
        P(None, None, "tensor"),
        P(None, None, "tensor"),
        P(("dp", "tensor"), None),
    )
    return jax.shard_map(
        on_device,
        mesh=mesh,
        in_specs=placed,
        out_specs=(
            P(("dp", "tensor"), None),
            P(("dp", "tensor"), None),
            P(),
            P(None, "dp", "tensor"),
            P("dp", "tensor"),
            P(),
            P(),
            P(),
            P(None, "dp", "tensor"),
            P(None, "dp", "tensor"),
        ),
        check_vma=False,
    )
```

```python
import functools
import jax, jax.numpy as jnp
from jax import lax
from jax.experimental import pallas as pl
from jax.experimental.pallas import tpu as pltpu
from jax.sharding import PartitionSpec as P

QB = 256
KB = 128


def mm(a, b, dims):
    return lax.dot_general(a, b, (dims, ((), ())), preferred_element_type=jnp.float32)


def score_block(keys, queries, skew, first_query, seq_len):
    scores = mm(keys, queries, ((1,), (0,)))
    bias = [
        skew[:, pl.ds(pl.multiple_of(first_query - first_key + seq_len - KB, KB), QB)]
        for first_key in range(0, seq_len, KB)
    ]
    return scores + jnp.concatenate(bias, axis=0)


def forward_kernel(seq_ref, qkv_ref, offset_ref, mixed_ref, lse_ref, skew):
    seq_len = qkv_ref.shape[2]
    scale = qkv_ref.shape[1] ** -0.5
    skew[...] = pltpu.roll(
        jnp.broadcast_to(offset_ref[0], (KB, 2 * seq_len)), 0, 1, stride=1, stride_axis=0
    )
    keys = qkv_ref[1].T
    values = qkv_ref[2]

    def block(index, carry):
        first = pl.multiple_of(index * QB, QB)
        queries = qkv_ref[0, :, pl.ds(first, QB)] * jnp.bfloat16(scale)
        scores = score_block(keys, queries, skew, first, seq_len)
        largest = jnp.max(scores, axis=0, keepdims=True)
        expos = jnp.exp(scores - largest)
        total = jnp.sum(expos, axis=0, keepdims=True)
        weights = (expos * (1.0 / total)).astype(jnp.bfloat16)
        mixed_ref[:, pl.ds(first, QB)] = mm(values, weights, ((1,), (0,))).astype(jnp.bfloat16)
        lse_ref[0, :, pl.ds(first, QB)] = largest + jnp.log(total)
        return carry

    lax.fori_loop(0, seq_len // QB, block, 0, unroll=True)


def forward_attention(seq, qkv, offsets, seq_len):
    _, width, rows = qkv.shape
    heads = offsets.shape[0]
    size = width // heads
    return pl.pallas_call(
        forward_kernel,
        grid_spec=pltpu.PrefetchScalarGridSpec(
            num_scalar_prefetch=1,
            grid=(heads,),
            in_specs=[
                pl.BlockSpec((3, size, seq_len), lambda h, s: (0, h, s[0])),
                pl.BlockSpec((1, 1, 2 * seq_len), lambda h, s: (h, 0, 0)),
            ],
            out_specs=[
                pl.BlockSpec((size, seq_len), lambda h, s: (h, 0)),
                pl.BlockSpec((1, 1, seq_len), lambda h, s: (h, 0, 0)),
            ],
            scratch_shapes=[pltpu.VMEM((KB, 2 * seq_len), jnp.float32)],
        ),
        out_shape=[
            jax.ShapeDtypeStruct((width, seq_len), jnp.bfloat16),
            jax.ShapeDtypeStruct((heads, 1, seq_len), jnp.float32),
        ],
        compiler_params=pltpu.CompilerParams(vmem_limit_bytes=48 * 2**20),
        cost_estimate=pl.CostEstimate(flops=1, bytes_accessed=1, transcendentals=0),
        name="attention_forward",
    )(seq, qkv, offsets)


def backward_kernel(
    seq_ref, qkv_ref, grad_ref, lse_ref, offset_ref, out_ref, diag_ref, skew, sums, probs_all, score_all
):
    seq_len = qkv_ref.shape[2]
    scale = qkv_ref.shape[1] ** -0.5
    skew[...] = pltpu.roll(
        jnp.broadcast_to(offset_ref[0], (KB, 2 * seq_len)), 0, 1, stride=1, stride_axis=0
    )
    sums[...] = jnp.zeros_like(sums)
    keys_t = qkv_ref[1]
    keys = keys_t.T
    values = qkv_ref[2].T

    def block(index, carry):
        first = pl.multiple_of(index * QB, QB)
        here = pl.ds(first, QB)
        queries = qkv_ref[0, :, here] * jnp.bfloat16(scale)
        scores = score_block(keys, queries, skew, first, seq_len)
        probs = jnp.exp(scores - lse_ref[0, :, here])
        probs_all[:, here] = probs.astype(jnp.bfloat16)
        prob_grad = mm(values, grad_ref[:, here], ((1,), (0,)))
        centre = jnp.sum(probs * prob_grad, axis=0, keepdims=True)
        score_grad = probs * (prob_grad - centre)
        rounded = score_grad.astype(jnp.bfloat16)
        score_all[:, here] = rounded
        for first_key in range(0, seq_len, KB):
            spot = pl.ds(pl.multiple_of(first - first_key + seq_len - KB, KB), QB)
            sums[:, spot] += score_grad[first_key : first_key + KB]
        out_ref[0, :, here] = (mm(keys_t, rounded, ((1,), (0,))) * scale).astype(jnp.bfloat16)
        return carry

    lax.fori_loop(0, seq_len // QB, block, 0, unroll=True)
    queries = qkv_ref[0] * jnp.bfloat16(scale)
    out_ref[1] = mm(queries, score_all[...], ((1,), (1,))).astype(jnp.bfloat16)
    out_ref[2] = mm(grad_ref[...], probs_all[...], ((1,), (1,))).astype(jnp.bfloat16)
    part = sums[...]
    half = KB // 2
    while half >= 1:
        part = part[:half] + pltpu.roll(part[half:], 2 * seq_len - half, 1)
        half //= 2
    diag_ref[0] = part


def backward_attention(seq, qkv, grads, lse, offsets, seq_len):
    _, width, rows = qkv.shape
    heads = offsets.shape[0]
    size = width // heads
    return pl.pallas_call(
        backward_kernel,
        grid_spec=pltpu.PrefetchScalarGridSpec(
            num_scalar_prefetch=1,
            grid=(heads,),
            in_specs=[
                pl.BlockSpec((3, size, seq_len), lambda h, s: (0, h, s[0])),
                pl.BlockSpec((size, seq_len), lambda h, s: (h, 0)),
                pl.BlockSpec((1, 1, seq_len), lambda h, s: (h, 0, 0)),
                pl.BlockSpec((1, 1, 2 * seq_len), lambda h, s: (h, 0, 0)),
            ],
            out_specs=[
                pl.BlockSpec((3, size, seq_len), lambda h, s: (0, h, 0)),
                pl.BlockSpec((1, 1, 2 * seq_len), lambda h, s: (h, 0, 0)),
            ],
            scratch_shapes=[
                pltpu.VMEM((KB, 2 * seq_len), jnp.float32),
                pltpu.VMEM((KB, 2 * seq_len), jnp.float32),
                pltpu.VMEM((seq_len, seq_len), jnp.bfloat16),
                pltpu.VMEM((seq_len, seq_len), jnp.bfloat16),
            ],
        ),
        out_shape=[
            jax.ShapeDtypeStruct((3, width, seq_len), jnp.bfloat16),
            jax.ShapeDtypeStruct((heads, 1, 2 * seq_len), jnp.float32),
        ],
        compiler_params=pltpu.CompilerParams(vmem_limit_bytes=48 * 2**20),
        cost_estimate=pl.CostEstimate(flops=1, bytes_accessed=1, transcendentals=0),
        name="attention_backward",
    )(seq, qkv, grads, lse, offsets)


CH = 16
UNIT = 128
FIELDS = 4


def unit_limit(rows, shares, experts):
    chunks = rows // CH + shares * (experts - 1)
    return (chunks + experts * (UNIT // CH - 1)) // (UNIT // CH)


def plan_segments(counts):
    starts = jnp.cumsum(counts, axis=1) - counts
    first = starts // CH
    chunks = jnp.where(counts > 0, (starts + counts + CH - 1) // CH - first, 0)
    units = (jnp.sum(chunks, axis=0) * CH + UNIT - 1) // UNIT
    base = jnp.cumsum(units) - units
    return jnp.concatenate(
        [first, chunks, starts, starts + counts, units[None], base[None]], axis=0
    ).astype(jnp.int32)


def for_units(units, step):
    def double(index, carry):
        step(index * (2 * UNIT), 2 * UNIT)
        return carry

    lax.fori_loop(0, units // 2, double, 0)

    @pl.when(units % 2 == 1)
    def _():
        step((units - 1) * UNIT, UNIT)


def at_rows(start, size):
    return pl.ds(pl.multiple_of(start, size if size < UNIT else UNIT), size)


def gather_rows(plan_ref, expert, shares, units, rows_refs, grad_refs, xs, cs, base):
    filled = 0
    for share in range(shares):
        first = plan_ref[share, expert]
        chunks = plan_ref[shares + share, expert]
        start = plan_ref[2 * shares + share, expert]
        end = plan_ref[3 * shares + share, expert]
        x_ref, c_ref = rows_refs[share], grad_refs[share]

        def gather(index, carry):
            here = (first + index) * CH
            local = (filled + index) * CH
            row = here + lax.broadcasted_iota(jnp.int32, (CH, 1), 0)
            keep = (row >= start) & (row < end)
            zero = jnp.zeros((), jnp.bfloat16)
            xs[at_rows(base + local, CH)] = jnp.where(keep, x_ref[at_rows(here, CH)], zero)
            cs[at_rows(local, CH)] = jnp.where(keep, c_ref[at_rows(here, CH)], zero)
            return carry

        lax.fori_loop(0, chunks, gather, 0)
        filled = filled + chunks

    def clear(index, carry):
        xs[at_rows(base + index * CH, CH)] = jnp.zeros((CH, xs.shape[1]), jnp.bfloat16)
        cs[at_rows(index * CH, CH)] = jnp.zeros((CH, cs.shape[1]), jnp.bfloat16)
        return carry

    lax.fori_loop(filled, units * (UNIT // CH), clear, 0)


def scatter_rows(plan_ref, expert, shares, buffers, outs):
    filled = 0
    for share in range(shares):
        first = plan_ref[share, expert]
        chunks = plan_ref[shares + share, expert]

        def scatter(index, carry):
            target = at_rows((first + index) * CH, CH)
            local = at_rows((filled + index) * CH, CH)
            for buffer, targets in zip(buffers, outs):
                out = targets[share]
                out[target] = (out[target].astype(jnp.float32) + buffer[local]).astype(out.dtype)
            return carry

        lax.fori_loop(0, chunks, scatter, 0)
        filled = filled + chunks


def store_parts(outs, slot, values, side, bit, piece):
    if len(outs) == 1:
        outs[0][slot] = values[...].astype(jnp.bfloat16)
        return
    for index in range(values.shape[0] // (2 * piece)):
        low, high = index % bit, index // bit
        for which, out in enumerate(outs):
            chosen = side if which == 0 else 1 - side
            start = ((high * 2 + chosen) * bit + low) * piece
            rows = values[pl.ds(pl.multiple_of(start, CH), piece)]
            out[slot, index] = rows.astype(jnp.bfloat16)


def expert_kernel(
    *refs, shares, first_expert, expert_count, with_grads, bits, piece, with_totals
):
    plan_ref, refs = refs[0], refs[1:]
    if with_grads:
        past_plan, side_ref, refs = refs[0], refs[1], refs[2:]
    x_refs, refs = refs[:shares], refs[shares:]
    c_refs, refs = refs[:shares], refs[shares:]
    router_ref, up_ref, down_ref, *refs = refs
    if with_grads:
        past, refs = refs[:4], refs[4:]
    if with_totals:
        totals, refs = refs[: 3 * shares], refs[3 * shares :]
    y_refs, refs = refs[:shares], refs[shares:]
    back_refs, refs = refs[:shares], refs[shares:]
    gate_refs, refs = refs[:shares], refs[shares:]
    if with_grads:
        parts = 2 if bits else 1
        up_outs, refs = refs[:parts], refs[parts:]
        down_outs, refs = refs[:parts], refs[parts:]
        xs, ms, dys, dus, *refs = refs
        cs, ybuf, bbuf, gbuf, *refs = refs
        gates, refs = refs[:shares], refs[shares:]
        old, up_acc, down_acc, sems = refs[:4], refs[4], refs[5], refs[6]
    else:
        xs, ms, dys, dus, cs, ybuf, bbuf, gbuf, *gates = refs
    step = pl.program_id(0)
    expert = step + first_expert
    units = plan_ref[4 * shares, expert]
    base = 0 if with_grads else plan_ref[4 * shares + 1, expert] * UNIT

    @pl.when(step == 0)
    def _():
        if with_totals:
            for out, total in zip((*y_refs, *back_refs), totals):
                out[...] = total[...]
        else:
            for out in (*y_refs, *back_refs):
                out[...] = jnp.zeros_like(out)
        for gate in gates:
            gate[...] = jnp.zeros_like(gate)

    if with_grads:
        past_units = past_plan[4 * shares, expert]
        past_base = past_plan[4 * shares + 1, expert] * UNIT

        def copies(index):
            return [
                pltpu.make_async_copy(
                    source.at[at_rows(past_base + index * UNIT, UNIT)],
                    target.at[at_rows(index * UNIT, UNIT)],
                    sems.at[which, index],
                )
                for which, (source, target) in enumerate(zip(past, old))
            ]

        def begin(index, carry):
            for copy in copies(index):
                copy.start()
            return carry

        def finish(index, carry):
            for copy in copies(index):
                copy.wait()
            return carry

        lax.fori_loop(0, past_units, begin, 0)

    gather_rows(plan_ref, expert, shares, units, x_refs, c_refs, xs, cs, base)

    def tile(start, size):
        local = at_rows(start, size)
        saved = at_rows(base + start, size)
        x = xs[saved]
        c = cs[local].astype(jnp.float32)
        logits = mm(x, router_ref[...], ((1,), (0,)))
        lane = lax.broadcasted_iota(jnp.int32, logits.shape, 1)
        logits = jnp.where(lane < expert_count, logits, -jnp.inf)
        expos = jnp.exp(logits - jnp.max(logits, axis=1, keepdims=True))
        mine = jnp.sum(jnp.where(lane == expert, expos, 0.0), axis=1, keepdims=True)
        gate = mine / jnp.sum(expos, axis=1, keepdims=True)
        dy = (gate * c).astype(jnp.bfloat16)
        dys[saved] = dy
        u = mm(x, up_ref[0], ((1,), (0,)))
        dm = mm(dy, down_ref[0], ((1,), (0,)))
        root = 0.7978845608028654
        square = u * u
        bent = jnp.tanh(root * (u * (1.0 + 0.044715 * square)))
        half = 0.5 * (1.0 + bent)
        m = (u * half).astype(jnp.bfloat16)
        ms[saved] = m
        slope = half + (0.5 * root) * (u * ((1.0 - bent * bent) * (1.0 + (3 * 0.044715) * square)))
        du = (slope * dm).astype(jnp.bfloat16)
        dus[saved] = du
        y = mm(m, down_ref[0], ((1,), (1,)))
        ybuf[local] = y
        gbuf[local] = jnp.broadcast_to(jnp.sum(y * c, axis=1, keepdims=True), (size, gbuf.shape[1]))
        bbuf[local] = mm(du, up_ref[0], ((1,), (1,)))

    for_units(units, tile)
    scatter_rows(
        plan_ref, expert, shares, (ybuf, bbuf, gbuf), (y_refs, back_refs, gates)
    )

    @pl.when(step == pl.num_programs(0) - 1)
    def _():
        for share in range(shares):
            row = gates[share][...].T[:1]
            gate_refs[share][...] = row + totals[2 * shares + share][...] if with_totals else row

    if with_grads:
        up_acc[...] = jnp.zeros_like(up_acc)
        down_acc[...] = jnp.zeros_like(down_acc)

        def add(arrays):
            def part(start, size):
                here = at_rows(start, size)
                x, m, dy, du = [array[here] for array in arrays]
                up_acc[...] += mm(x, du, ((0,), (0,)))
                down_acc[...] += mm(dy, m, ((0,), (0,)))

            return part

        for_units(units, add((xs, ms, dys, dus)))
        lax.fori_loop(0, past_units, finish, 0)
        for_units(past_units, add(old))
        up_bit, down_bit = bits or (0, 0)
        store_parts(up_outs, 0, up_acc, side_ref[0], up_bit, piece)
        store_parts(down_outs, 0, down_acc, side_ref[1], down_bit, piece)


def run_experts(plan, x, c, router, up, down, past=None, first_expert=0, step_count=None):
    shares = len(x)
    rows, width = x[0].shape
    experts, _, hidden = up.shape
    steps = step_count or experts
    with_grads = past is not None
    saved = unit_limit(rows * shares, shares, experts) * UNIT
    most = rows * shares
    brain, full = jnp.bfloat16, jnp.float32
    whole = lambda shape: pl.BlockSpec(shape, lambda e, *p: (0, 0))
    block = pl.BlockSpec((1, width, hidden), lambda e, *p: (first_expert + e, 0, 0))
    scalars = [plan]
    inputs = [*x, *c, router, up, down]
    in_specs = [whole((rows, width))] * (2 * shares) + [whole(router.shape), block, block]
    row_types = [full] + [brain] * (shares - 1)
    out_shape = [jax.ShapeDtypeStruct((rows, width), kind) for kind in row_types * 2]
    out_specs = [whole((rows, width))] * (2 * shares) + [whole((1, rows))] * shares
    out_shape += [jax.ShapeDtypeStruct((1, rows), full)] * shares
    scratch = [
        pltpu.VMEM((most, width), brain),
        pltpu.VMEM((most, width), full),
        pltpu.VMEM((most, width), full),
        pltpu.VMEM((most, 128), full),
    ] + [pltpu.VMEM((rows, 128), full)] * shares
    widths = (width, hidden, width, hidden)
    if with_grads:
        past_plan, past_arrays, sides, bits, piece, totals = past
        scalars += [past_plan, sides]
        inputs += past_arrays
        in_specs += [pl.BlockSpec(memory_space=pl.ANY)] * 4
        inputs += totals
        in_specs += [whole(array.shape) for array in totals]
        if bits:
            shape = (width // (2 * piece), piece, hidden)
            out_specs += [pl.BlockSpec((1, *shape), lambda e, *p: (e, 0, 0, 0))] * 4
            out_shape += [jax.ShapeDtypeStruct((steps, *shape), brain)] * 4
        else:
            out_specs += [pl.BlockSpec((1, width, hidden), lambda e, *p: (e, 0, 0))] * 2
            out_shape += [jax.ShapeDtypeStruct((steps, width, hidden), brain)] * 2
        buffers = [pltpu.VMEM((most, size), brain) for size in widths]
        scratch = (
            buffers
            + scratch
            + buffers
            + [pltpu.VMEM((width, hidden), full)] * 2
            + [pltpu.SemaphoreType.DMA((4, most // UNIT))]
        )
    else:
        out_specs += [whole((saved, size)) for size in widths]
        out_shape += [jax.ShapeDtypeStruct((saved, size), brain) for size in widths]
    return pl.pallas_call(
        functools.partial(
            expert_kernel,
            shares=shares,
            first_expert=first_expert,
            expert_count=experts,
            with_grads=with_grads,
            bits=bits if with_grads else None,
            piece=piece if with_grads else None,
            with_totals=with_grads and len(totals) > 0,
        ),
        grid_spec=pltpu.PrefetchScalarGridSpec(
            num_scalar_prefetch=len(scalars),
            grid=(steps,),
            in_specs=in_specs,
            out_specs=out_specs,
            scratch_shapes=scratch,
        ),
        out_shape=out_shape,
        compiler_params=pltpu.CompilerParams(vmem_limit_bytes=58 * 2**20),
        cost_estimate=pl.CostEstimate(flops=1, bytes_accessed=1, transcendentals=0),
        name="experts_and_grads" if with_grads else "experts",
    )(*scalars, *inputs)


def input_kernel(core_ref, grad_ref, weight_ref, keep_ref, send_ref):
    share = keep_ref.shape[0]
    for target, out in ((core_ref[0], keep_ref), (1 - core_ref[0], send_ref)):
        here = pl.ds(pl.multiple_of(target * share, share), share)
        total = sum(
            mm(grad_ref[which, :, here].T, weight_ref[which], ((1,), (0,))) for which in range(3)
        )
        out[...] = total.astype(out.dtype)


def input_grads(core, qkv_rows, qkv_weight):
    share = qkv_rows.shape[2] // 2
    width = qkv_weight.shape[2]
    vmem = pl.BlockSpec(memory_space=pltpu.VMEM)
    return pl.pallas_call(
        input_kernel,
        in_specs=[pl.BlockSpec(memory_space=pltpu.SMEM), vmem, vmem],
        out_specs=[vmem, vmem],
        out_shape=[
            jax.ShapeDtypeStruct((share, width), jnp.float32),
            jax.ShapeDtypeStruct((share, width), jnp.bfloat16),
        ],
        compiler_params=pltpu.CompilerParams(vmem_limit_bytes=40 * 2**20),
        name="input_grads",
    )(core, qkv_rows, qkv_weight)


def projection_kernel(*refs, bit, piece):
    side, *refs = refs
    (rows_a, rows_b, grad_a, grad_b, out_a, out_b, mixed_a, mixed_b, weight, *outs) = refs
    *outs, gain, part_ref = outs
    gain_total = jnp.zeros(gain.shape, jnp.float32)
    for which in range(4):
        if which < 3:
            part = mm(grad_a[which], rows_a[...], ((1,), (0,)))
            part = part + mm(grad_b[which], rows_b[...], ((1,), (0,)))
            turned = weight[which].astype(jnp.float32)
            gain_total = gain_total + jnp.sum(turned * part, axis=0, keepdims=True)
        else:
            part = mm(mixed_a[...], out_a[...], ((1,), (0,)))
            part = part + mm(mixed_b[...], out_b[...], ((1,), (0,)))
        part_ref[...] = part.T
        store_parts(outs, which, part_ref, side[0], bit, piece)
    gain[...] = gain_total


def projection_grads(side, normed, qkv_rows, out_rows, mixed, qkv_weight, bit, piece):
    _, size, seq_len = qkv_rows[0].shape
    width = normed[0].shape[1]
    whole = lambda shape: pl.BlockSpec(shape, lambda i, *p: (0,) * len(shape))
    operands = [*normed, *qkv_rows, *out_rows, *mixed, qkv_weight]
    in_specs = [whole(array.shape) for array in operands]
    if bit:
        shapes = [(4, width // (2 * piece), piece, size)] * 2
    else:
        shapes = [(4, width, size)]
    out_shape = [jax.ShapeDtypeStruct(shape, jnp.bfloat16) for shape in shapes]
    out_shape += [jax.ShapeDtypeStruct((1, width), jnp.float32)]
    return pl.pallas_call(
        functools.partial(projection_kernel, bit=bit, piece=piece),
        grid_spec=pltpu.PrefetchScalarGridSpec(
            num_scalar_prefetch=1,
            grid=(1,),
            in_specs=in_specs,
            out_specs=[whole(array.shape) for array in out_shape],
            scratch_shapes=[pltpu.VMEM((width, size), jnp.float32)],
        ),
        out_shape=out_shape,
        compiler_params=pltpu.CompilerParams(vmem_limit_bytes=56 * 2**20),
        name="projection_grads",
    )(side, *operands)


EPS = 1e-06
F32 = jnp.float32
BF16 = jnp.bfloat16


def norm_rows(values, gain_vector):
    return values * lax.rsqrt(jnp.mean(values * values, axis=-1, keepdims=True) + EPS) * gain_vector


def swap(values, axis, bit):
    count = lax.axis_size(axis)
    return lax.ppermute(values, axis, [(i, i ^ bit) for i in range(count)])


def after(value, *milestones):
    return lax.optimization_barrier((value, milestones))[0]


def join(values, *moving):
    values, landed = lax.optimization_barrier((values, tuple(move.moving for move in moving)))
    for move, received in zip(moving, landed):
        move.moving = received
    return values


class Transfer:
    def __init__(self, values, axis, bit):
        self.moving = swap(values, axis, bit)


class ScatterSum:
    def __init__(self, parts, bits):
        self.bits = list(bits)
        self.left = sorted(bits, reverse=True)
        self.moving = None
        self.parts = None
        experts, width = parts[0].shape[0], parts[0].shape[-1]
        sizes = [2] * len(self.bits)
        if len(parts) == 1:
            values = parts[0]
            self.values = values.reshape(experts, *sizes, values.shape[1] >> len(sizes), width)
        else:
            self.parts = parts
            self.shape = (experts, *sizes[1:], parts[0].shape[-2], width)

    def pick(self, other):
        mine = (lax.axis_index("dp") // self.bit) % 2
        index = 1 - mine if other else mine
        return lax.dynamic_index_in_dim(self.values, index, self.spot, keepdims=False)

    def land(self):
        keep = self.parts[0] if self.parts else self.pick(False)
        self.values = keep.astype(F32) + self.moving.astype(F32)
        if self.parts:
            self.values = self.values.reshape(self.shape)
        self.parts = None
        self.moving = None
        self.left.remove(self.bit)

    def launch(self, *milestones):
        if self.moving is not None:
            self.land()
        if not self.bits:
            return
        self.bit = self.bits.pop(0)
        self.spot = 1 + self.left.index(self.bit)
        if self.parts:
            self.sent = after(self.parts[1], *milestones) if milestones else self.parts[1]
        else:
            self.values = after(self.values, *milestones) if milestones else self.values
            self.sent = self.pick(True).astype(BF16)
        self.moving = swap(self.sent, "dp", self.bit)

    def finish(self):
        while self.moving is not None:
            self.launch()
        return self.values


def sum_along(values, steps):
    for axis, bit in steps:
        values = values + swap(values, axis, bit)
    return values


def on_device(
    tokens,
    attn_gain,
    qkv_weight,
    proj_weight,
    bias_table,
    buckets,
    ffn_gain,
    router_weight,
    routes,
    up_weight,
    down_weight,
    cotangent,
):
    highest = lax.Precision.HIGHEST
    rank = lax.axis_index("tensor")
    core, chip = rank % 2, rank // 2
    tensor_count = lax.axis_size("tensor")
    rows, width = tokens.shape
    share = rows // tensor_count
    half = rows // 2
    seq_len = (buckets.shape[0] + 1) // 2
    heads, bucket_count = bias_table.shape
    experts = up_weight.shape[0]
    zero_seq = jnp.zeros((1,), jnp.int32)

    flipped = buckets[::-1]
    cut = KB - 1
    turned = jnp.concatenate([flipped[cut:], jnp.full((1,), -1, flipped.dtype), flipped[:cut]])
    bucket_hot = (turned[:, None] == jnp.arange(bucket_count)[None, :]).astype(F32)
    offsets = jnp.dot(bias_table, bucket_hot.T, precision=highest)[:, None, :]

    all_routes = routes[:, 0].reshape(tensor_count, share)
    counts = jnp.sum((all_routes[:, :, None] == jnp.arange(experts)).astype(jnp.int32), axis=1)
    order = rank ^ jnp.arange(tensor_count)
    same = order[:, None] == jnp.arange(tensor_count)[None, :]
    counts = jnp.sum(jnp.where(same[:, :, None], counts[None], 0), axis=1)
    my_routes = lax.dynamic_slice_in_dim(routes[:, 0], rank * share, share, 0)
    my_hot = (my_routes[:, None] == jnp.arange(experts)[None, :]).astype(F32)
    earlier = (jnp.arange(share)[:, None] > jnp.arange(share)[None, :]).astype(BF16)
    ahead = jnp.dot(earlier, my_hot.astype(BF16), preferred_element_type=F32)
    starts = (jnp.cumsum(counts[0]) - counts[0]).astype(F32)
    position = jnp.sum(my_hot * (ahead + starts[None, :]), axis=1).astype(jnp.int32)
    place = jnp.arange(share)[:, None] == position[None, :]
    place_matrix = place.astype(BF16)

    def sort_rows(values):
        return jnp.dot(place_matrix, values, preferred_element_type=F32).astype(BF16)

    def unsort_rows(values):
        dims = (((0,), (0,)), ((), ()))
        high = lax.reduce_precision(values, 8, 7)
        low = (values - high).astype(BF16)
        return lax.dot_general(
            place_matrix, high.astype(BF16), dims, preferred_element_type=F32
        ) + lax.dot_general(place_matrix, low, dims, preferred_element_type=F32)

    grad_mine = sort_rows(cotangent)
    grad_near = swap(grad_mine, "tensor", 1)
    grad_far = Transfer(grad_mine, "tensor", 2)
    early = (grad_mine, grad_near, place_matrix, my_hot)
    input_share = lax.dynamic_slice_in_dim(tokens, rank * share, share, 0).astype(F32)

    def project_rows(which, *milestones):
        inputs = lax.dynamic_slice_in_dim(after(tokens, *milestones), which * half, half, 0)
        normed = norm_rows(inputs.astype(F32), attn_gain).astype(BF16)
        qkv = jnp.einsum("cdf,td->cft", qkv_weight, normed, preferred_element_type=F32)
        return normed, qkv.astype(BF16)

    normed_other, qkv_other = project_rows(1 - chip, *early)

    def columns(values, core_index):
        return lax.dynamic_slice_in_dim(values, core_index * share, share, values.ndim - 1)

    def project(mixed, core_index):
        return jnp.einsum(
            "ft,df->td", columns(mixed, core_index), proj_weight, preferred_element_type=F32
        )

    mixed_other, lse_other = join(
        forward_attention(zero_seq, qkv_other, offsets, seq_len), grad_far
    )
    for_near = project(mixed_other, 1 - core).astype(BF16)
    passed = swap(for_near, "tensor", 1)
    normed_own, qkv_own = project_rows(chip, for_near)
    kept = project(after(mixed_other, qkv_own), core)
    attn_sent = (kept + passed.astype(F32)).astype(BF16)
    attn_far = Transfer(attn_sent, "tensor", 2)
    grad_far = grad_far.moving
    grad_both = swap(grad_far, "tensor", 1)
    own_attention = forward_attention(
        after(zero_seq, attn_sent, grad_both), qkv_own, offsets, seq_len
    )
    late_counts, late_router = after((counts, router_weight), qkv_own)
    own_plan = plan_segments(late_counts[:2])
    other_plan = plan_segments(late_counts[2:])
    padded_router = jnp.pad(late_router, ((0, 0), (0, 128 - experts)))
    (mixed_own, lse_own), own_plan, other_plan, padded_router = join(
        (own_attention, own_plan, other_plan, padded_router), attn_far
    )
    attn_near = swap(project(mixed_own, 1 - core).astype(BF16), "tensor", 1)
    attn_share = project(mixed_own, core) + attn_near.astype(F32) + attn_far.moving.astype(F32)
    hidden_share = input_share + attn_share
    normed_two = norm_rows(hidden_share, ffn_gain).astype(BF16)

    rows_mine = sort_rows(normed_two)
    rows_far = Transfer(rows_mine, "tensor", 2)
    rows_near = swap(rows_mine, "tensor", 1)
    own = run_experts(
        own_plan, [rows_mine, rows_near], [grad_mine, grad_near], padded_router, up_weight, down_weight
    )
    own = join(own, rows_far)
    count = lax.axis_size("dp")
    index = lax.axis_index("dp")
    bits = [1 << i for i in range(count.bit_length() - 1)]
    turned_bits = bits[1:] + bits[:1]
    piece = width // count
    aligned = piece % CH == 0
    back_near = swap(own[3], "tensor", 1)
    gate_near = swap(own[5][0], "tensor", 1)
    rows_far = rows_far.moving
    other_rows = [rows_far, swap(rows_far, "tensor", 1)]
    split = experts // 2

    def run_other(plan, start, firsts, totals):
        sides = jnp.stack([index // bit % 2 for bit in firsts]).astype(jnp.int32)
        past = (own_plan, own[6:], sides, firsts if aligned else None, piece, totals)
        return run_experts(
            plan, other_rows, [grad_far, grad_both], padded_router, up_weight, down_weight,
            past, start, split,
        )

    parts = 2 if aligned else 1
    first = run_other(
        after(other_plan, back_near, gate_near), 0, (turned_bits[0], bits[0]), []
    )
    down_one = ScatterSum(first[6 + parts :], bits)
    up_one = ScatterSum(first[6 : 6 + parts], turned_bits)
    down_one.launch()
    up_one.launch()
    second = join(
        run_other(
            after(other_plan, down_one.sent, up_one.sent), split, (bits[0], bits[0]), []
        ),
        down_one,
        up_one,
    )
    other = [one.astype(F32) + two.astype(F32) for one, two in zip(first[:6], second[:6])]
    back_passed = swap(other[3].astype(BF16), "tensor", 1)
    gate_passed = swap(other[5][0], "tensor", 1)
    back_sent = (other[2] + back_passed.astype(F32)).astype(BF16)
    gate_far = Transfer(other[4][0] + gate_passed, "tensor", 2)
    back_far = Transfer(back_sent, "tensor", 2)
    down_two = ScatterSum(second[6 + parts :], bits)
    up_two = ScatterSum(second[6 : 6 + parts], bits)
    down_two.launch()
    up_one.launch()
    down_one.moving = after(down_one.moving, back_sent)
    down_one.launch()
    back_far = join(back_far.moving, down_two, down_one, up_one, gate_far)
    gate_sorted = own[4][0] + gate_near + gate_far.moving
    back_share = unsort_rows(own[2] + back_near.astype(F32) + back_far.astype(F32))
    gate_grad = jnp.sum(jnp.where(place, gate_sorted[:, None], 0.0), axis=0)

    logits = jnp.dot(normed_two, router_weight, preferred_element_type=F32)
    router_probs = jax.nn.softmax(logits, axis=-1)
    gate_prob = jnp.sum(router_probs * my_hot, axis=-1)
    grad_out = cotangent.astype(F32)
    logit_grad = ((gate_grad * gate_prob)[:, None] * (my_hot - router_probs)).astype(BF16)
    router_grad = jnp.einsum("td,te->de", normed_two, logit_grad, preferred_element_type=F32)
    normed_grad = back_share + jnp.einsum(
        "te,de->td", logit_grad, router_weight, preferred_element_type=F32
    )
    hidden_part, ffn_gain_grad = jax.vjp(norm_rows, hidden_share, ffn_gain)[1](normed_grad)
    hidden_grad = grad_out + hidden_part

    attn_grad = hidden_grad.astype(BF16)
    far_grad = Transfer(attn_grad, "tensor", 2)
    near_grad = swap(attn_grad, "tensor", 1)
    up_two.launch(attn_grad)
    down_two.moving, down_one.moving = after((down_two.moving, down_one.moving), attn_grad)
    down_two.launch()
    down_one.launch()

    def in_order(mine, partner):
        return jnp.concatenate(
            [jnp.where(core == 0, mine, partner), jnp.where(core == 0, partner, mine)]
        )

    def mixed_grad(rows_grad):
        return jnp.einsum("df,td->ft", proj_weight, rows_grad, preferred_element_type=F32).astype(
            BF16
        )

    own_attn_grad = in_order(attn_grad, near_grad)
    own_mixed_grad = after(mixed_grad(own_attn_grad), up_two.sent, down_one.sent, down_two.sent)
    own_qkv_grad, own_diag = join(
        backward_attention(zero_seq, qkv_own, own_mixed_grad, lse_own, offsets, seq_len),
        far_grad,
        up_two,
        down_one,
        down_two,
    )
    far_grad = far_grad.moving
    other_attn_grad = in_order(far_grad, swap(far_grad, "tensor", 1))
    held = after((own[0], own[1], other[0], other[1]), own_qkv_grad)
    out_near = swap(held[1], "tensor", 1)
    out_passed = swap(held[3].astype(BF16), "tensor", 1)
    out_sent = (held[2] + out_passed.astype(F32)).astype(BF16)
    out_far = Transfer(out_sent, "tensor", 2)
    up_one.moving, down_two.moving = after((up_one.moving, down_two.moving), own_qkv_grad)
    up_one.launch()
    down_two.launch()
    up_two.launch()
    other_mixed_grad = after(
        mixed_grad(other_attn_grad), out_sent, out_near, up_one.sent, down_two.sent, up_two.sent
    )
    other_qkv_grad, other_diag = join(
        backward_attention(zero_seq, qkv_other, other_mixed_grad, lse_other, offsets, seq_len),
        out_far,
        up_one,
        down_two,
        up_two,
    )
    out_far = out_far.moving

    core_index = core.astype(jnp.int32).reshape(1)
    turned_weight = qkv_weight.swapaxes(1, 2)
    up_two.launch()
    normed_own, own_late = after((normed_own, own_qkv_grad), up_two.sent)
    *qkv_proj, gain_part = projection_grads(
        (index // bits[0] % 2).astype(jnp.int32).reshape(1),
        (normed_own, normed_other),
        (own_late, other_qkv_grad),
        (own_attn_grad, other_attn_grad),
        (mixed_own, mixed_other),
        turned_weight,
        bits[0] if aligned else 0,
        piece,
    )
    projections = ScatterSum(qkv_proj, bits)
    projections.launch()
    input_keep, input_send = input_grads(
        after(core_index, projections.sent), other_qkv_grad, turned_weight
    )
    input_passed = swap(input_send, "tensor", 1)
    input_sent = (input_keep + input_passed.astype(F32)).astype(BF16)
    input_far = Transfer(input_sent, "tensor", 2)
    input_own, input_send = input_grads(after(core_index, input_sent), own_late, turned_weight)
    input_near = swap(input_send, "tensor", 1)
    attn_gain_grad = gain_part[0] / attn_gain
    table_local = jnp.dot((own_diag + other_diag)[:, 0], bucket_hot, precision=highest)
    table_full = lax.dynamic_update_slice_in_dim(
        jnp.zeros((heads * tensor_count, bucket_count), F32), table_local, rank * heads, 0
    )
    small = [attn_gain_grad, ffn_gain_grad, router_grad.reshape(-1), table_full.reshape(-1)]
    sizes = [array.size for array in small]
    packed = jnp.concatenate(small)
    packed = jnp.pad(packed, (0, -packed.size % 1024)).reshape(-1, 128)
    late, packed = join(after((input_own, packed), input_near), projections, up_two)
    projections.launch()
    packed = after(packed, projections.sent)
    packed = sum_along(packed, [("tensor", 1), ("dp", bits[0])])
    packed = join(packed, projections)
    projections.launch()
    late = join(after(late, projections.sent), input_far)
    packed = after(packed, projections.sent)
    input_share_grad = late + input_near.astype(F32) + input_far.moving.astype(F32)
    token_part = jax.vjp(lambda rows_in: norm_rows(rows_in, attn_gain), input_share)[1](
        input_share_grad
    )[0]
    tokens_grad = hidden_grad + token_part

    expert_share = unsort_rows(held[0] + out_near.astype(F32) + out_far.astype(F32))
    layer_out = (hidden_share + gate_prob[:, None] * expert_share).astype(BF16)

    packed = sum_along(packed, [("tensor", 2)] + [("dp", bit) for bit in bits[1:]]).reshape(-1)
    ends = [sum(sizes[:i]) for i in range(5)]
    attn_gain_grad, ffn_gain_grad, router_grad, table_grad = [
        packed[ends[i] : ends[i + 1]] for i in range(4)
    ]
    down_grad = jnp.concatenate([down_one.finish(), down_two.finish()])
    up_grad = jnp.concatenate([up_one.finish(), up_two.finish()])
    qkv_proj = projections.finish()
    return (
        layer_out,
        tokens_grad,
        attn_gain_grad,
        qkv_proj[:3],
        qkv_proj[3],
        table_grad.reshape(heads * tensor_count, bucket_count),
        ffn_gain_grad,
        router_grad.reshape(router_weight.shape),
        up_grad,
        down_grad,
    )


def solution(mesh):
    placed = (
        P("dp", None),
        P(),
        P(None, None, "tensor"),
        P(None, "tensor"),
        P("tensor", None),
        P(),
        P(),
        P(),
        P("dp", None),
        P(None, None, "tensor"),
        P(None, None, "tensor"),
        P(("dp", "tensor"), None),
    )
    return jax.shard_map(
        on_device,
        mesh=mesh,
        in_specs=placed,
        out_specs=(
            P(("dp", "tensor"), None),
            P(("dp", "tensor"), None),
            P(),
            P(None, "dp", "tensor"),
            P("dp", "tensor"),
            P(),
            P(),
            P(),
            P(None, "dp", "tensor"),
            P(None, "dp", "tensor"),
        ),
        check_vma=False,
    )
```

```python
import functools
import jax, jax.numpy as jnp
from jax import lax
from jax.experimental import pallas as pl
from jax.experimental.pallas import tpu as pltpu
from jax.sharding import PartitionSpec as P

QB = 512
KB = 128


def mm(a, b, dims):
    return lax.dot_general(a, b, (dims, ((), ())), preferred_element_type=jnp.float32)


def score_block(keys, queries, skew, first_query, seq_len):
    scores = mm(keys, queries, ((1,), (0,)))
    bias = [
        skew[:, pl.ds(pl.multiple_of(first_query - first_key + seq_len - KB, KB), QB)]
        for first_key in range(0, seq_len, KB)
    ]
    return scores + jnp.concatenate(bias, axis=0)


def forward_kernel(seq_ref, qkv_ref, offset_ref, mixed_ref, lse_ref, skew):
    seq_len = qkv_ref.shape[2]
    scale = qkv_ref.shape[1] ** -0.5
    skew[...] = pltpu.roll(
        jnp.broadcast_to(offset_ref[0], (KB, 2 * seq_len)), 0, 1, stride=1, stride_axis=0
    )
    keys = qkv_ref[1].T
    values = qkv_ref[2]

    def block(index, carry):
        first = pl.multiple_of(index * QB, QB)
        queries = qkv_ref[0, :, pl.ds(first, QB)] * jnp.bfloat16(scale)
        scores = score_block(keys, queries, skew, first, seq_len)
        largest = jnp.max(scores, axis=0, keepdims=True)
        expos = jnp.exp(scores - largest)
        total = jnp.sum(expos, axis=0, keepdims=True)
        weights = (expos * (1.0 / total)).astype(jnp.bfloat16)
        mixed_ref[:, pl.ds(first, QB)] = mm(values, weights, ((1,), (0,))).astype(jnp.bfloat16)
        lse_ref[0, :, pl.ds(first, QB)] = largest + jnp.log(total)
        return carry

    lax.fori_loop(0, seq_len // QB, block, 0, unroll=True)


def forward_attention(seq, qkv, offsets, seq_len):
    _, width, rows = qkv.shape
    heads = offsets.shape[0]
    size = width // heads
    return pl.pallas_call(
        forward_kernel,
        grid_spec=pltpu.PrefetchScalarGridSpec(
            num_scalar_prefetch=1,
            grid=(heads,),
            in_specs=[
                pl.BlockSpec((3, size, seq_len), lambda h, s: (0, h, s[0])),
                pl.BlockSpec((1, 1, 2 * seq_len), lambda h, s: (h, 0, 0)),
            ],
            out_specs=[
                pl.BlockSpec((size, seq_len), lambda h, s: (h, 0)),
                pl.BlockSpec((1, 1, seq_len), lambda h, s: (h, 0, 0)),
            ],
            scratch_shapes=[pltpu.VMEM((KB, 2 * seq_len), jnp.float32)],
        ),
        out_shape=[
            jax.ShapeDtypeStruct((width, seq_len), jnp.bfloat16),
            jax.ShapeDtypeStruct((heads, 1, seq_len), jnp.float32),
        ],
        compiler_params=pltpu.CompilerParams(vmem_limit_bytes=48 * 2**20),
        cost_estimate=pl.CostEstimate(flops=1, bytes_accessed=1, transcendentals=0),
        name="attention_forward",
    )(seq, qkv, offsets)


def backward_kernel(
    seq_ref, qkv_ref, grad_ref, lse_ref, offset_ref, out_ref, diag_ref, skew, sums, probs_all, score_all
):
    seq_len = qkv_ref.shape[2]
    scale = qkv_ref.shape[1] ** -0.5
    skew[...] = pltpu.roll(
        jnp.broadcast_to(offset_ref[0], (KB, 2 * seq_len)), 0, 1, stride=1, stride_axis=0
    )
    sums[...] = jnp.zeros_like(sums)
    keys_t = qkv_ref[1]
    keys = keys_t.T
    values = qkv_ref[2].T

    def block(index, carry):
        first = pl.multiple_of(index * QB, QB)
        here = pl.ds(first, QB)
        queries = qkv_ref[0, :, here] * jnp.bfloat16(scale)
        scores = score_block(keys, queries, skew, first, seq_len)
        probs = jnp.exp(scores - lse_ref[0, :, here])
        probs_all[:, here] = probs.astype(jnp.bfloat16)
        prob_grad = mm(values, grad_ref[:, here], ((1,), (0,)))
        centre = jnp.sum(probs * prob_grad, axis=0, keepdims=True)
        score_grad = probs * (prob_grad - centre)
        rounded = score_grad.astype(jnp.bfloat16)
        score_all[:, here] = rounded
        for first_key in range(0, seq_len, KB):
            spot = pl.ds(pl.multiple_of(first - first_key + seq_len - KB, KB), QB)
            sums[:, spot] += score_grad[first_key : first_key + KB]
        out_ref[0, :, here] = (mm(keys_t, rounded, ((1,), (0,))) * scale).astype(jnp.bfloat16)
        return carry

    lax.fori_loop(0, seq_len // QB, block, 0, unroll=True)
    queries = qkv_ref[0] * jnp.bfloat16(scale)
    out_ref[1] = mm(queries, score_all[...], ((1,), (1,))).astype(jnp.bfloat16)
    out_ref[2] = mm(grad_ref[...], probs_all[...], ((1,), (1,))).astype(jnp.bfloat16)
    part = sums[...]
    half = KB // 2
    while half >= 1:
        part = part[:half] + pltpu.roll(part[half:], 2 * seq_len - half, 1)
        half //= 2
    diag_ref[0] = part


def backward_attention(seq, qkv, grads, lse, offsets, seq_len):
    _, width, rows = qkv.shape
    heads = offsets.shape[0]
    size = width // heads
    return pl.pallas_call(
        backward_kernel,
        grid_spec=pltpu.PrefetchScalarGridSpec(
            num_scalar_prefetch=1,
            grid=(heads,),
            in_specs=[
                pl.BlockSpec((3, size, seq_len), lambda h, s: (0, h, s[0])),
                pl.BlockSpec((size, seq_len), lambda h, s: (h, 0)),
                pl.BlockSpec((1, 1, seq_len), lambda h, s: (h, 0, 0)),
                pl.BlockSpec((1, 1, 2 * seq_len), lambda h, s: (h, 0, 0)),
            ],
            out_specs=[
                pl.BlockSpec((3, size, seq_len), lambda h, s: (0, h, 0)),
                pl.BlockSpec((1, 1, 2 * seq_len), lambda h, s: (h, 0, 0)),
            ],
            scratch_shapes=[
                pltpu.VMEM((KB, 2 * seq_len), jnp.float32),
                pltpu.VMEM((KB, 2 * seq_len), jnp.float32),
                pltpu.VMEM((seq_len, seq_len), jnp.bfloat16),
                pltpu.VMEM((seq_len, seq_len), jnp.bfloat16),
            ],
        ),
        out_shape=[
            jax.ShapeDtypeStruct((3, width, seq_len), jnp.bfloat16),
            jax.ShapeDtypeStruct((heads, 1, 2 * seq_len), jnp.float32),
        ],
        compiler_params=pltpu.CompilerParams(vmem_limit_bytes=48 * 2**20),
        cost_estimate=pl.CostEstimate(flops=1, bytes_accessed=1, transcendentals=0),
        name="attention_backward",
    )(seq, qkv, grads, lse, offsets)


CH = 16
UNIT = 128
FIELDS = 4


def unit_limit(rows, shares, experts):
    chunks = rows // CH + shares * (experts - 1)
    return (chunks + experts * (UNIT // CH - 1)) // (UNIT // CH)


def plan_segments(counts):
    starts = jnp.cumsum(counts, axis=1) - counts
    first = starts // CH
    chunks = jnp.where(counts > 0, (starts + counts + CH - 1) // CH - first, 0)
    units = (jnp.sum(chunks, axis=0) * CH + UNIT - 1) // UNIT
    base = jnp.cumsum(units) - units
    return jnp.concatenate(
        [first, chunks, starts, starts + counts, units[None], base[None]], axis=0
    ).astype(jnp.int32)


def for_units(units, step):
    def double(index, carry):
        step(index * (2 * UNIT), 2 * UNIT)
        return carry

    lax.fori_loop(0, units // 2, double, 0)

    @pl.when(units % 2 == 1)
    def _():
        step((units - 1) * UNIT, UNIT)


def at_rows(start, size):
    return pl.ds(pl.multiple_of(start, size if size < UNIT else UNIT), size)


def gather_rows(plan_ref, expert, shares, units, rows_refs, grad_refs, xs, cs, base):
    filled = 0
    for share in range(shares):
        first = plan_ref[share, expert]
        chunks = plan_ref[shares + share, expert]
        start = plan_ref[2 * shares + share, expert]
        end = plan_ref[3 * shares + share, expert]
        x_ref, c_ref = rows_refs[share], grad_refs[share]

        def gather(index, carry):
            here = (first + index) * CH
            local = (filled + index) * CH
            row = here + lax.broadcasted_iota(jnp.int32, (CH, 1), 0)
            keep = (row >= start) & (row < end)
            zero = jnp.zeros((), jnp.bfloat16)
            xs[at_rows(base + local, CH)] = jnp.where(keep, x_ref[at_rows(here, CH)], zero)
            cs[at_rows(local, CH)] = jnp.where(keep, c_ref[at_rows(here, CH)], zero)
            return carry

        lax.fori_loop(0, chunks, gather, 0)
        filled = filled + chunks

    def clear(index, carry):
        xs[at_rows(base + index * CH, CH)] = jnp.zeros((CH, xs.shape[1]), jnp.bfloat16)
        cs[at_rows(index * CH, CH)] = jnp.zeros((CH, cs.shape[1]), jnp.bfloat16)
        return carry

    lax.fori_loop(filled, units * (UNIT // CH), clear, 0)


def scatter_rows(plan_ref, expert, shares, buffers, outs):
    filled = 0
    for share in range(shares):
        first = plan_ref[share, expert]
        chunks = plan_ref[shares + share, expert]

        def scatter(index, carry):
            target = at_rows((first + index) * CH, CH)
            local = at_rows((filled + index) * CH, CH)
            for buffer, targets in zip(buffers, outs):
                out = targets[share]
                out[target] = (out[target].astype(jnp.float32) + buffer[local]).astype(out.dtype)
            return carry

        lax.fori_loop(0, chunks, scatter, 0)
        filled = filled + chunks


def store_parts(outs, slot, values, side, bit, piece):
    if len(outs) == 1:
        outs[0][slot] = values[...].astype(jnp.bfloat16)
        return
    for index in range(values.shape[0] // (2 * piece)):
        low, high = index % bit, index // bit
        for which, out in enumerate(outs):
            chosen = side if which == 0 else 1 - side
            start = ((high * 2 + chosen) * bit + low) * piece
            rows = values[pl.ds(pl.multiple_of(start, CH), piece)]
            out[slot, index] = rows.astype(jnp.bfloat16)


def expert_kernel(
    *refs, shares, first_expert, expert_count, with_grads, bits, piece, with_totals
):
    plan_ref, refs = refs[0], refs[1:]
    if with_grads:
        past_plan, side_ref, refs = refs[0], refs[1], refs[2:]
    x_refs, refs = refs[:shares], refs[shares:]
    c_refs, refs = refs[:shares], refs[shares:]
    router_ref, up_ref, down_ref, *refs = refs
    if with_grads:
        past, refs = refs[:4], refs[4:]
    if with_totals:
        totals, refs = refs[: 3 * shares], refs[3 * shares :]
    y_refs, refs = refs[:shares], refs[shares:]
    back_refs, refs = refs[:shares], refs[shares:]
    gate_refs, refs = refs[:shares], refs[shares:]
    if with_grads:
        parts = 2 if bits else 1
        up_outs, refs = refs[:parts], refs[parts:]
        down_outs, refs = refs[:parts], refs[parts:]
        xs, ms, dys, dus, *refs = refs
        cs, ybuf, bbuf, gbuf, *refs = refs
        gates, refs = refs[:shares], refs[shares:]
        old, up_acc, down_acc, sems = refs[:4], refs[4], refs[5], refs[6]
    else:
        xs, ms, dys, dus, cs, ybuf, bbuf, gbuf, *gates = refs
    step = pl.program_id(0)
    expert = step + first_expert
    units = plan_ref[4 * shares, expert]
    base = 0 if with_grads else plan_ref[4 * shares + 1, expert] * UNIT

    @pl.when(step == 0)
    def _():
        if with_totals:
            for out, total in zip((*y_refs, *back_refs), totals):
                out[...] = total[...]
        else:
            for out in (*y_refs, *back_refs):
                out[...] = jnp.zeros_like(out)
        for gate in gates:
            gate[...] = jnp.zeros_like(gate)

    if with_grads:
        past_units = past_plan[4 * shares, expert]
        past_base = past_plan[4 * shares + 1, expert] * UNIT

        def copies(index):
            return [
                pltpu.make_async_copy(
                    source.at[at_rows(past_base + index * UNIT, UNIT)],
                    target.at[at_rows(index * UNIT, UNIT)],
                    sems.at[which, index],
                )
                for which, (source, target) in enumerate(zip(past, old))
            ]

        def begin(index, carry):
            for copy in copies(index):
                copy.start()
            return carry

        def finish(index, carry):
            for copy in copies(index):
                copy.wait()
            return carry

        lax.fori_loop(0, past_units, begin, 0)

    gather_rows(plan_ref, expert, shares, units, x_refs, c_refs, xs, cs, base)

    def tile(start, size):
        local = at_rows(start, size)
        saved = at_rows(base + start, size)
        x = xs[saved]
        c = cs[local].astype(jnp.float32)
        logits = mm(x, router_ref[...], ((1,), (0,)))
        lane = lax.broadcasted_iota(jnp.int32, logits.shape, 1)
        logits = jnp.where(lane < expert_count, logits, -jnp.inf)
        expos = jnp.exp(logits - jnp.max(logits, axis=1, keepdims=True))
        mine = jnp.sum(jnp.where(lane == expert, expos, 0.0), axis=1, keepdims=True)
        gate = mine / jnp.sum(expos, axis=1, keepdims=True)
        dy = (gate * c).astype(jnp.bfloat16)
        dys[saved] = dy
        u = mm(x, up_ref[0], ((1,), (0,)))
        dm = mm(dy, down_ref[0], ((1,), (0,)))
        root = 0.7978845608028654
        square = u * u
        bent = jnp.tanh(root * (u * (1.0 + 0.044715 * square)))
        half = 0.5 * (1.0 + bent)
        m = (u * half).astype(jnp.bfloat16)
        ms[saved] = m
        slope = half + (0.5 * root) * (u * ((1.0 - bent * bent) * (1.0 + (3 * 0.044715) * square)))
        du = (slope * dm).astype(jnp.bfloat16)
        dus[saved] = du
        y = mm(m, down_ref[0], ((1,), (1,)))
        ybuf[local] = y
        gbuf[local] = jnp.broadcast_to(jnp.sum(y * c, axis=1, keepdims=True), (size, gbuf.shape[1]))
        bbuf[local] = mm(du, up_ref[0], ((1,), (1,)))

    for_units(units, tile)
    scatter_rows(
        plan_ref, expert, shares, (ybuf, bbuf, gbuf), (y_refs, back_refs, gates)
    )

    @pl.when(step == pl.num_programs(0) - 1)
    def _():
        for share in range(shares):
            row = gates[share][...].T[:1]
            gate_refs[share][...] = row + totals[2 * shares + share][...] if with_totals else row

    if with_grads:
        up_acc[...] = jnp.zeros_like(up_acc)
        down_acc[...] = jnp.zeros_like(down_acc)

        def add(arrays):
            def part(start, size):
                here = at_rows(start, size)
                x, m, dy, du = [array[here] for array in arrays]
                up_acc[...] += mm(x, du, ((0,), (0,)))
                down_acc[...] += mm(dy, m, ((0,), (0,)))

            return part

        for_units(units, add((xs, ms, dys, dus)))
        lax.fori_loop(0, past_units, finish, 0)
        for_units(past_units, add(old))
        up_bit, down_bit = bits or (0, 0)
        store_parts(up_outs, 0, up_acc, side_ref[0], up_bit, piece)
        store_parts(down_outs, 0, down_acc, side_ref[1], down_bit, piece)


def run_experts(plan, x, c, router, up, down, past=None, first_expert=0, step_count=None):
    shares = len(x)
    rows, width = x[0].shape
    experts, _, hidden = up.shape
    steps = step_count or experts
    with_grads = past is not None
    saved = unit_limit(rows * shares, shares, experts) * UNIT
    most = rows * shares
    brain, full = jnp.bfloat16, jnp.float32
    whole = lambda shape: pl.BlockSpec(shape, lambda e, *p: (0, 0))
    block = pl.BlockSpec((1, width, hidden), lambda e, *p: (first_expert + e, 0, 0))
    scalars = [plan]
    inputs = [*x, *c, router, up, down]
    in_specs = [whole((rows, width))] * (2 * shares) + [whole(router.shape), block, block]
    row_types = [full] + [brain] * (shares - 1)
    out_shape = [jax.ShapeDtypeStruct((rows, width), kind) for kind in row_types * 2]
    out_specs = [whole((rows, width))] * (2 * shares) + [whole((1, rows))] * shares
    out_shape += [jax.ShapeDtypeStruct((1, rows), full)] * shares
    scratch = [
        pltpu.VMEM((most, width), brain),
        pltpu.VMEM((most, width), full),
        pltpu.VMEM((most, width), full),
        pltpu.VMEM((most, 128), full),
    ] + [pltpu.VMEM((rows, 128), full)] * shares
    widths = (width, hidden, width, hidden)
    if with_grads:
        past_plan, past_arrays, sides, bits, piece, totals = past
        scalars += [past_plan, sides]
        inputs += past_arrays
        in_specs += [pl.BlockSpec(memory_space=pl.ANY)] * 4
        inputs += totals
        in_specs += [whole(array.shape) for array in totals]
        if bits:
            shape = (width // (2 * piece), piece, hidden)
            out_specs += [pl.BlockSpec((1, *shape), lambda e, *p: (e, 0, 0, 0))] * 4
            out_shape += [jax.ShapeDtypeStruct((steps, *shape), brain)] * 4
        else:
            out_specs += [pl.BlockSpec((1, width, hidden), lambda e, *p: (e, 0, 0))] * 2
            out_shape += [jax.ShapeDtypeStruct((steps, width, hidden), brain)] * 2
        buffers = [pltpu.VMEM((most, size), brain) for size in widths]
        scratch = (
            buffers
            + scratch
            + buffers
            + [pltpu.VMEM((width, hidden), full)] * 2
            + [pltpu.SemaphoreType.DMA((4, most // UNIT))]
        )
    else:
        out_specs += [whole((saved, size)) for size in widths]
        out_shape += [jax.ShapeDtypeStruct((saved, size), brain) for size in widths]
    return pl.pallas_call(
        functools.partial(
            expert_kernel,
            shares=shares,
            first_expert=first_expert,
            expert_count=experts,
            with_grads=with_grads,
            bits=bits if with_grads else None,
            piece=piece if with_grads else None,
            with_totals=with_grads and len(totals) > 0,
        ),
        grid_spec=pltpu.PrefetchScalarGridSpec(
            num_scalar_prefetch=len(scalars),
            grid=(steps,),
            in_specs=in_specs,
            out_specs=out_specs,
            scratch_shapes=scratch,
        ),
        out_shape=out_shape,
        compiler_params=pltpu.CompilerParams(vmem_limit_bytes=58 * 2**20),
        cost_estimate=pl.CostEstimate(flops=1, bytes_accessed=1, transcendentals=0),
        name="experts_and_grads" if with_grads else "experts",
    )(*scalars, *inputs)


def input_kernel(core_ref, grad_ref, weight_ref, keep_ref, send_ref):
    share = keep_ref.shape[0]
    for target, out in ((core_ref[0], keep_ref), (1 - core_ref[0], send_ref)):
        here = pl.ds(pl.multiple_of(target * share, share), share)
        total = sum(
            mm(grad_ref[which, :, here].T, weight_ref[which], ((1,), (0,))) for which in range(3)
        )
        out[...] = total.astype(out.dtype)


def input_grads(core, qkv_rows, qkv_weight):
    share = qkv_rows.shape[2] // 2
    width = qkv_weight.shape[2]
    vmem = pl.BlockSpec(memory_space=pltpu.VMEM)
    return pl.pallas_call(
        input_kernel,
        in_specs=[pl.BlockSpec(memory_space=pltpu.SMEM), vmem, vmem],
        out_specs=[vmem, vmem],
        out_shape=[
            jax.ShapeDtypeStruct((share, width), jnp.float32),
            jax.ShapeDtypeStruct((share, width), jnp.bfloat16),
        ],
        compiler_params=pltpu.CompilerParams(vmem_limit_bytes=40 * 2**20),
        name="input_grads",
    )(core, qkv_rows, qkv_weight)


def projection_kernel(*refs, bit, piece):
    side, *refs = refs
    (rows_a, rows_b, grad_a, grad_b, out_a, out_b, mixed_a, mixed_b, weight, *outs) = refs
    *outs, gain, part_ref = outs
    gain_total = jnp.zeros(gain.shape, jnp.float32)
    for which in range(4):
        if which < 3:
            part = mm(grad_a[which], rows_a[...], ((1,), (0,)))
            part = part + mm(grad_b[which], rows_b[...], ((1,), (0,)))
            turned = weight[which].astype(jnp.float32)
            gain_total = gain_total + jnp.sum(turned * part, axis=0, keepdims=True)
        else:
            part = mm(mixed_a[...], out_a[...], ((1,), (0,)))
            part = part + mm(mixed_b[...], out_b[...], ((1,), (0,)))
        part_ref[...] = part.T
        store_parts(outs, which, part_ref, side[0], bit, piece)
    gain[...] = gain_total


def projection_grads(side, normed, qkv_rows, out_rows, mixed, qkv_weight, bit, piece):
    _, size, seq_len = qkv_rows[0].shape
    width = normed[0].shape[1]
    whole = lambda shape: pl.BlockSpec(shape, lambda i, *p: (0,) * len(shape))
    operands = [*normed, *qkv_rows, *out_rows, *mixed, qkv_weight]
    in_specs = [whole(array.shape) for array in operands]
    if bit:
        shapes = [(4, width // (2 * piece), piece, size)] * 2
    else:
        shapes = [(4, width, size)]
    out_shape = [jax.ShapeDtypeStruct(shape, jnp.bfloat16) for shape in shapes]
    out_shape += [jax.ShapeDtypeStruct((1, width), jnp.float32)]
    return pl.pallas_call(
        functools.partial(projection_kernel, bit=bit, piece=piece),
        grid_spec=pltpu.PrefetchScalarGridSpec(
            num_scalar_prefetch=1,
            grid=(1,),
            in_specs=in_specs,
            out_specs=[whole(array.shape) for array in out_shape],
            scratch_shapes=[pltpu.VMEM((width, size), jnp.float32)],
        ),
        out_shape=out_shape,
        compiler_params=pltpu.CompilerParams(vmem_limit_bytes=56 * 2**20),
        name="projection_grads",
    )(side, *operands)


EPS = 1e-06
F32 = jnp.float32
BF16 = jnp.bfloat16


def norm_rows(values, gain_vector):
    return values * lax.rsqrt(jnp.mean(values * values, axis=-1, keepdims=True) + EPS) * gain_vector


def swap(values, axis, bit):
    count = lax.axis_size(axis)
    return lax.ppermute(values, axis, [(i, i ^ bit) for i in range(count)])


def after(value, *milestones):
    return lax.optimization_barrier((value, milestones))[0]


def join(values, *moving):
    values, landed = lax.optimization_barrier((values, tuple(move.moving for move in moving)))
    for move, received in zip(moving, landed):
        move.moving = received
    return values


class Transfer:
    def __init__(self, values, axis, bit):
        self.moving = swap(values, axis, bit)


class ScatterSum:
    def __init__(self, parts, bits):
        self.bits = list(bits)
        self.left = sorted(bits, reverse=True)
        self.moving = None
        self.parts = None
        experts, width = parts[0].shape[0], parts[0].shape[-1]
        sizes = [2] * len(self.bits)
        if len(parts) == 1:
            values = parts[0]
            self.values = values.reshape(experts, *sizes, values.shape[1] >> len(sizes), width)
        else:
            self.parts = parts
            self.shape = (experts, *sizes[1:], parts[0].shape[-2], width)

    def pick(self, other):
        mine = (lax.axis_index("dp") // self.bit) % 2
        index = 1 - mine if other else mine
        return lax.dynamic_index_in_dim(self.values, index, self.spot, keepdims=False)

    def land(self):
        keep = self.parts[0] if self.parts else self.pick(False)
        self.values = keep.astype(F32) + self.moving.astype(F32)
        if self.parts:
            self.values = self.values.reshape(self.shape)
        self.parts = None
        self.moving = None
        self.left.remove(self.bit)

    def launch(self, *milestones):
        if self.moving is not None:
            self.land()
        if not self.bits:
            return
        self.bit = self.bits.pop(0)
        self.spot = 1 + self.left.index(self.bit)
        if self.parts:
            self.sent = after(self.parts[1], *milestones) if milestones else self.parts[1]
        else:
            self.values = after(self.values, *milestones) if milestones else self.values
            self.sent = self.pick(True).astype(BF16)
        self.moving = swap(self.sent, "dp", self.bit)

    def finish(self):
        while self.moving is not None:
            self.launch()
        return self.values


def sum_along(values, steps):
    for axis, bit in steps:
        values = values + swap(values, axis, bit)
    return values


def on_device(
    tokens,
    attn_gain,
    qkv_weight,
    proj_weight,
    bias_table,
    buckets,
    ffn_gain,
    router_weight,
    routes,
    up_weight,
    down_weight,
    cotangent,
):
    highest = lax.Precision.HIGHEST
    rank = lax.axis_index("tensor")
    core, chip = rank % 2, rank // 2
    tensor_count = lax.axis_size("tensor")
    rows, width = tokens.shape
    share = rows // tensor_count
    half = rows // 2
    seq_len = (buckets.shape[0] + 1) // 2
    heads, bucket_count = bias_table.shape
    experts = up_weight.shape[0]
    zero_seq = jnp.zeros((1,), jnp.int32)

    flipped = buckets[::-1]
    cut = KB - 1
    turned = jnp.concatenate([flipped[cut:], jnp.full((1,), -1, flipped.dtype), flipped[:cut]])
    bucket_hot = (turned[:, None] == jnp.arange(bucket_count)[None, :]).astype(F32)
    offsets = jnp.dot(bias_table, bucket_hot.T, precision=highest)[:, None, :]

    all_routes = routes[:, 0].reshape(tensor_count, share)
    counts = jnp.sum((all_routes[:, :, None] == jnp.arange(experts)).astype(jnp.int32), axis=1)
    order = rank ^ jnp.arange(tensor_count)
    same = order[:, None] == jnp.arange(tensor_count)[None, :]
    counts = jnp.sum(jnp.where(same[:, :, None], counts[None], 0), axis=1)
    my_routes = lax.dynamic_slice_in_dim(routes[:, 0], rank * share, share, 0)
    my_hot = (my_routes[:, None] == jnp.arange(experts)[None, :]).astype(F32)
    earlier = (jnp.arange(share)[:, None] > jnp.arange(share)[None, :]).astype(BF16)
    ahead = jnp.dot(earlier, my_hot.astype(BF16), preferred_element_type=F32)
    starts = (jnp.cumsum(counts[0]) - counts[0]).astype(F32)
    position = jnp.sum(my_hot * (ahead + starts[None, :]), axis=1).astype(jnp.int32)
    place = jnp.arange(share)[:, None] == position[None, :]
    place_matrix = place.astype(BF16)

    def sort_rows(values):
        return jnp.dot(place_matrix, values, preferred_element_type=F32).astype(BF16)

    def unsort_rows(values):
        dims = (((0,), (0,)), ((), ()))
        high = lax.reduce_precision(values, 8, 7)
        low = (values - high).astype(BF16)
        return lax.dot_general(
            place_matrix, high.astype(BF16), dims, preferred_element_type=F32
        ) + lax.dot_general(place_matrix, low, dims, preferred_element_type=F32)

    grad_mine = sort_rows(cotangent)
    grad_near = swap(grad_mine, "tensor", 1)
    grad_far = Transfer(grad_mine, "tensor", 2)
    early = (grad_mine, grad_near, place_matrix, my_hot)
    input_share = lax.dynamic_slice_in_dim(tokens, rank * share, share, 0).astype(F32)

    def project_rows(which, *milestones):
        inputs = lax.dynamic_slice_in_dim(after(tokens, *milestones), which * half, half, 0)
        normed = norm_rows(inputs.astype(F32), attn_gain).astype(BF16)
        qkv = jnp.einsum("cdf,td->cft", qkv_weight, normed, preferred_element_type=F32)
        return normed, qkv.astype(BF16)

    normed_other, qkv_other = project_rows(1 - chip, *early)

    def columns(values, core_index):
        return lax.dynamic_slice_in_dim(values, core_index * share, share, values.ndim - 1)

    def project(mixed, core_index):
        return jnp.einsum(
            "ft,df->td", columns(mixed, core_index), proj_weight, preferred_element_type=F32
        )

    mixed_other, lse_other = join(
        forward_attention(zero_seq, qkv_other, offsets, seq_len), grad_far
    )
    for_near = project(mixed_other, 1 - core).astype(BF16)
    passed = swap(for_near, "tensor", 1)
    normed_own, qkv_own = project_rows(chip, for_near)
    kept = project(after(mixed_other, qkv_own), core)
    attn_sent = (kept + passed.astype(F32)).astype(BF16)
    attn_far = Transfer(attn_sent, "tensor", 2)
    grad_far = grad_far.moving
    grad_both = swap(grad_far, "tensor", 1)
    own_attention = forward_attention(
        after(zero_seq, attn_sent, grad_both), qkv_own, offsets, seq_len
    )
    late_counts, late_router = after((counts, router_weight), qkv_own)
    own_plan = plan_segments(late_counts[:2])
    other_plan = plan_segments(late_counts[2:])
    padded_router = jnp.pad(late_router, ((0, 0), (0, 128 - experts)))
    (mixed_own, lse_own), own_plan, other_plan, padded_router = join(
        (own_attention, own_plan, other_plan, padded_router), attn_far
    )
    attn_near = swap(project(mixed_own, 1 - core).astype(BF16), "tensor", 1)
    attn_share = project(mixed_own, core) + attn_near.astype(F32) + attn_far.moving.astype(F32)
    hidden_share = input_share + attn_share
    normed_two = norm_rows(hidden_share, ffn_gain).astype(BF16)

    rows_mine = sort_rows(normed_two)
    rows_far = Transfer(rows_mine, "tensor", 2)
    rows_near = swap(rows_mine, "tensor", 1)
    own = run_experts(
        own_plan, [rows_mine, rows_near], [grad_mine, grad_near], padded_router, up_weight, down_weight
    )
    own = join(own, rows_far)
    count = lax.axis_size("dp")
    index = lax.axis_index("dp")
    bits = [1 << i for i in range(count.bit_length() - 1)]
    turned_bits = bits[1:] + bits[:1]
    piece = width // count
    aligned = piece % CH == 0
    back_near = swap(own[3], "tensor", 1)
    gate_near = swap(own[5][0], "tensor", 1)
    rows_far = rows_far.moving
    other_rows = [rows_far, swap(rows_far, "tensor", 1)]
    split = experts // 2

    def run_other(plan, start, firsts, totals):
        sides = jnp.stack([index // bit % 2 for bit in firsts]).astype(jnp.int32)
        past = (own_plan, own[6:], sides, firsts if aligned else None, piece, totals)
        return run_experts(
            plan, other_rows, [grad_far, grad_both], padded_router, up_weight, down_weight,
            past, start, split,
        )

    parts = 2 if aligned else 1
    first = run_other(
        after(other_plan, back_near, gate_near), 0, (turned_bits[0], bits[0]), []
    )
    down_one = ScatterSum(first[6 + parts :], bits)
    up_one = ScatterSum(first[6 : 6 + parts], turned_bits)
    down_one.launch()
    up_one.launch()
    second = join(
        run_other(
            after(other_plan, down_one.sent, up_one.sent), split, (bits[0], bits[0]), []
        ),
        down_one,
        up_one,
    )
    other = [one.astype(F32) + two.astype(F32) for one, two in zip(first[:6], second[:6])]
    back_passed = swap(other[3].astype(BF16), "tensor", 1)
    gate_passed = swap(other[5][0], "tensor", 1)
    back_sent = (other[2] + back_passed.astype(F32)).astype(BF16)
    gate_far = Transfer(other[4][0] + gate_passed, "tensor", 2)
    back_far = Transfer(back_sent, "tensor", 2)
    down_two = ScatterSum(second[6 + parts :], bits)
    up_two = ScatterSum(second[6 : 6 + parts], bits)
    down_two.launch()
    up_one.launch()
    down_one.moving = after(down_one.moving, back_sent)
    down_one.launch()
    back_far = join(back_far.moving, down_two, down_one, up_one, gate_far)
    gate_sorted = own[4][0] + gate_near + gate_far.moving
    back_share = unsort_rows(own[2] + back_near.astype(F32) + back_far.astype(F32))
    gate_grad = jnp.sum(jnp.where(place, gate_sorted[:, None], 0.0), axis=0)

    logits = jnp.dot(normed_two, router_weight, preferred_element_type=F32)
    router_probs = jax.nn.softmax(logits, axis=-1)
    gate_prob = jnp.sum(router_probs * my_hot, axis=-1)
    grad_out = cotangent.astype(F32)
    logit_grad = ((gate_grad * gate_prob)[:, None] * (my_hot - router_probs)).astype(BF16)
    router_grad = jnp.einsum("td,te->de", normed_two, logit_grad, preferred_element_type=F32)
    normed_grad = back_share + jnp.einsum(
        "te,de->td", logit_grad, router_weight, preferred_element_type=F32
    )
    hidden_part, ffn_gain_grad = jax.vjp(norm_rows, hidden_share, ffn_gain)[1](normed_grad)
    hidden_grad = grad_out + hidden_part

    attn_grad = hidden_grad.astype(BF16)
    far_grad = Transfer(attn_grad, "tensor", 2)
    near_grad = swap(attn_grad, "tensor", 1)
    up_two.launch(attn_grad)
    down_two.moving, down_one.moving = after((down_two.moving, down_one.moving), attn_grad)
    down_two.launch()
    down_one.launch()

    def in_order(mine, partner):
        return jnp.concatenate(
            [jnp.where(core == 0, mine, partner), jnp.where(core == 0, partner, mine)]
        )

    def mixed_grad(rows_grad):
        return jnp.einsum("df,td->ft", proj_weight, rows_grad, preferred_element_type=F32).astype(
            BF16
        )

    own_attn_grad = in_order(attn_grad, near_grad)
    own_mixed_grad = after(mixed_grad(own_attn_grad), up_two.sent, down_one.sent, down_two.sent)
    own_qkv_grad, own_diag = join(
        backward_attention(zero_seq, qkv_own, own_mixed_grad, lse_own, offsets, seq_len),
        far_grad,
        up_two,
        down_one,
        down_two,
    )
    far_grad = far_grad.moving
    other_attn_grad = in_order(far_grad, swap(far_grad, "tensor", 1))
    held = after((own[0], own[1], other[0], other[1]), own_qkv_grad)
    out_near = swap(held[1], "tensor", 1)
    out_passed = swap(held[3].astype(BF16), "tensor", 1)
    out_sent = (held[2] + out_passed.astype(F32)).astype(BF16)
    out_far = Transfer(out_sent, "tensor", 2)
    up_one.moving, down_two.moving = after((up_one.moving, down_two.moving), own_qkv_grad)
    up_one.launch()
    down_two.launch()
    up_two.launch()
    other_mixed_grad = after(
        mixed_grad(other_attn_grad), out_sent, out_near, up_one.sent, down_two.sent, up_two.sent
    )
    other_qkv_grad, other_diag = join(
        backward_attention(zero_seq, qkv_other, other_mixed_grad, lse_other, offsets, seq_len),
        out_far,
        up_one,
        down_two,
        up_two,
    )
    out_far = out_far.moving

    core_index = core.astype(jnp.int32).reshape(1)
    turned_weight = qkv_weight.swapaxes(1, 2)
    up_two.launch()
    normed_own, own_late = after((normed_own, own_qkv_grad), up_two.sent)
    *qkv_proj, gain_part = projection_grads(
        (index // bits[0] % 2).astype(jnp.int32).reshape(1),
        (normed_own, normed_other),
        (own_late, other_qkv_grad),
        (own_attn_grad, other_attn_grad),
        (mixed_own, mixed_other),
        turned_weight,
        bits[0] if aligned else 0,
        piece,
    )
    projections = ScatterSum(qkv_proj, bits)
    projections.launch()
    input_keep, input_send = input_grads(
        after(core_index, projections.sent), other_qkv_grad, turned_weight
    )
    input_passed = swap(input_send, "tensor", 1)
    input_sent = (input_keep + input_passed.astype(F32)).astype(BF16)
    input_far = Transfer(input_sent, "tensor", 2)
    input_own, input_send = input_grads(after(core_index, input_sent), own_late, turned_weight)
    input_near = swap(input_send, "tensor", 1)
    attn_gain_grad = gain_part[0] / attn_gain
    table_local = jnp.dot((own_diag + other_diag)[:, 0], bucket_hot, precision=highest)
    table_full = lax.dynamic_update_slice_in_dim(
        jnp.zeros((heads * tensor_count, bucket_count), F32), table_local, rank * heads, 0
    )
    small = [attn_gain_grad, ffn_gain_grad, router_grad.reshape(-1), table_full.reshape(-1)]
    sizes = [array.size for array in small]
    packed = jnp.concatenate(small)
    packed = jnp.pad(packed, (0, -packed.size % 1024)).reshape(-1, 128)
    late, packed = join(after((input_own, packed), input_near), projections, up_two)
    projections.launch()
    packed = after(packed, projections.sent)
    packed = sum_along(packed, [("tensor", 1), ("dp", bits[0])])
    packed = join(packed, projections)
    projections.launch()
    late = join(after(late, projections.sent), input_far)
    packed = after(packed, projections.sent)
    input_share_grad = late + input_near.astype(F32) + input_far.moving.astype(F32)
    token_part = jax.vjp(lambda rows_in: norm_rows(rows_in, attn_gain), input_share)[1](
        input_share_grad
    )[0]
    tokens_grad = hidden_grad + token_part

    expert_share = unsort_rows(held[0] + out_near.astype(F32) + out_far.astype(F32))
    layer_out = (hidden_share + gate_prob[:, None] * expert_share).astype(BF16)

    packed = sum_along(packed, [("tensor", 2)] + [("dp", bit) for bit in bits[1:]]).reshape(-1)
    ends = [sum(sizes[:i]) for i in range(5)]
    attn_gain_grad, ffn_gain_grad, router_grad, table_grad = [
        packed[ends[i] : ends[i + 1]] for i in range(4)
    ]
    down_grad = jnp.concatenate([down_one.finish(), down_two.finish()])
    up_grad = jnp.concatenate([up_one.finish(), up_two.finish()])
    qkv_proj = projections.finish()
    return (
        layer_out,
        tokens_grad,
        attn_gain_grad,
        qkv_proj[:3],
        qkv_proj[3],
        table_grad.reshape(heads * tensor_count, bucket_count),
        ffn_gain_grad,
        router_grad.reshape(router_weight.shape),
        up_grad,
        down_grad,
    )


def solution(mesh):
    placed = (
        P("dp", None),
        P(),
        P(None, None, "tensor"),
        P(None, "tensor"),
        P("tensor", None),
        P(),
        P(),
        P(),
        P("dp", None),
        P(None, None, "tensor"),
        P(None, None, "tensor"),
        P(("dp", "tensor"), None),
    )
    return jax.shard_map(
        on_device,
        mesh=mesh,
        in_specs=placed,
        out_specs=(
            P(("dp", "tensor"), None),
            P(("dp", "tensor"), None),
            P(),
            P(None, "dp", "tensor"),
            P("dp", "tensor"),
            P(),
            P(),
            P(),
            P(None, "dp", "tensor"),
            P(None, "dp", "tensor"),
        ),
        check_vma=False,
    )
```
